32 devices in a mesh: groups: 2 (over y), fsdp: 4 (over z), tp: 4 (over x, core).
Axes of the slice: x: 2, y: 2, z: 4, core: 2. Of those that a mesh axis runs over, the one named last changes fastest.
Arguments:
- learner_weight: bfloat16 [16384, 2048], P(('groups', 'fsdp', 'tp')), parts along dimension 0, may hold values from -1 to 1
- hidden_states: bfloat16 [8, 16, 8192], P('groups', 'fsdp'), parts along dimension 0, may hold values from -6 to 6
- queries: bfloat16 [8, 16, 8192], P('groups', 'fsdp', 'tp'), parts along dimension 0, may hold values from -31 to 31
- cache_keys: bfloat16 [96, 512, 1024], P(('groups', 'fsdp'), None, 'tp'), parts along dimension 0, may hold values from -6 to 6
- cache_values: bfloat16 [96, 512, 1024], P(('groups', 'fsdp'), None, 'tp'), parts along dimension 0, may hold values from -6 to 6
- block_table: int32 [32, 3], P(('groups', 'fsdp')), parts along dimension 0, may hold values from 0 to 11, as said below
- lengths: int32 [32], P(('groups', 'fsdp')), parts along dimension 0, may hold values from 1 to 1536, as said below
Outputs:
- new_entries: bfloat16 [8, 16, 2048], P('groups', 'fsdp', 'tp'), parts along dimension 0
- attended: bfloat16 [8, 16, 8192], P('groups', 'fsdp', 'tp'), parts along dimension 0
The draws below stay inside these ranges and needn't reach their ends.
There are 2 independent parts, one for each index of `groups`. The reference program is written for one: setup_inputs(seed, part) draws one part's arguments, and reference() takes and returns one part's arrays. A program takes and returns all parts, laid end to end along the dimension named above; each array names one. Nothing has to cross between parts.
Inputs may be any that keep to these rules, and one draw needn't show every extreme that they name: `block_table`: within the 4 rows of one replica, the 12 entries are a permutation of that replica's 12 local slots; entries of blocks past a row's length are not read. `lengths`: in every replica at least one row holds exactly 1536 tokens.
All inputs are finite; a program needn't handle non-finite values.
Results may differ from the reference program's by a relative error of at most 0.02.
Values may be sent and summed in bfloat16 or wider, within the bound.
No kernel may reach another device: no remote copies, remote signals or barrier semaphores. Data moves between devices by JAX's collectives and lax.ppermute only.
A program may use at most 192 MiB of HBM per device.

```python
import math
import jax
import jax.numpy as jnp
from jax import lax

D = 8192
QH = 64
KVH = 8
HD = 128
STEPS = 4
BLOCK = 512
MAXB = 3
ROWS_DEV = 4
POOL = 12
ROWS = 16
SLOTS = 48


def layout(key):
    key = jax.random.fold_in(key, 11)
    first, second, third = jax.random.split(key, 3)
    replicas = ROWS // ROWS_DEV
    orders = jax.vmap(lambda item: jax.random.permutation(item, POOL))(jax.random.split(first, replicas))
    table = orders.reshape(ROWS, MAXB).astype(jnp.int32)
    drawn = jax.random.randint(second, (ROWS,), 1, MAXB * BLOCK + 1)
    longest = jax.random.randint(third, (replicas,), 0, ROWS_DEV)
    marked = jnp.arange(ROWS) % ROWS_DEV == jnp.repeat(longest, ROWS_DEV)
    lengths = jnp.where(marked, MAXB * BLOCK, drawn).astype(jnp.int32)
    return (table, lengths)


def draw_learner_weight(key, part):
    key = jax.random.fold_in(key, 17)
    keys = jax.random.split(key, 7)
    width = 2 * KVH
    codes = jax.random.randint(keys[0], (D, width, HD), 1, 15).astype(jnp.float32)
    offset = jax.random.uniform(keys[1], (D, width, HD), jnp.float32, 0.12, 0.36)
    flips = jnp.where(jax.random.bernoulli(keys[2], 0.5, (D, width, HD)), 1.0, -1.0)
    low_spot = jax.random.randint(keys[3], (D, width, 1), 0, HD)
    high_spot = (low_spot + jax.random.randint(keys[4], (D, width, 1), 1, HD)) % HD
    position = jnp.arange(HD, dtype=jnp.int32)[None, None, :]
    level = codes + offset * flips
    level = jnp.where(position == low_spot, 0.0, level)
    level = jnp.where(position == high_spot, 15.0, level)
    scale = 1.5 * jnp.exp(jax.random.uniform(keys[5], (D, width, 1), jnp.float32, 0.0, 0.98))
    centre = jax.random.uniform(keys[6], (D, width, 1), jnp.float32, -0.3, 0.3)
    spread = scale * D ** (-0.5)
    weight = spread * (centre + (level - 7.5) / 7.5)
    return weight.reshape(D, width * HD).astype(jnp.bfloat16)


def draw_block_table(key, part):
    table, lengths = layout(key)
    return table


def draw_lengths(key, part):
    table, lengths = layout(key)
    return lengths


def draw_cache_keys(key, part):
    key = jax.random.fold_in(key, 5)
    keys = jnp.clip(jax.random.normal(key, (SLOTS, BLOCK, KVH * HD), jnp.float32), -6.0, 6.0)
    return keys.astype(jnp.bfloat16)


def draw_queries(key, part):
    key = jax.random.fold_in(key, 7)
    first = jax.random.fold_in(key, 0)
    values = jnp.clip(2.0 * jax.random.normal(first, (STEPS, ROWS, QH * HD), jnp.float32), -8.0, 8.0)
    return values.astype(jnp.bfloat16)


def steps_of(rng, extent, pieces, smallest, largest):
    gain, own = 1.0, jax.random.fold_in(rng, 6)
    for dim, blocks in pieces:
        draws = jnp.exp(jax.random.uniform(jax.random.fold_in(own, dim), (blocks,), jnp.float32, smallest / len(pieces), largest / len(pieces)))
        gain = gain * jnp.repeat(draws, extent[dim] // blocks).reshape([-1 if axis == dim else 1 for axis in range(len(extent))])
    return gain


def scatter_about(key, extent, deviation, most, cuts=(), kind=jnp.bfloat16):
    result = jax.random.normal(key, extent, jnp.float32) * deviation
    if len(cuts) > 0:
        result = steps_of(key, extent, cuts, -0.22, 0.18) * result
    return jnp.clip(result, min=-most, max=most).astype(kind)


def setup_inputs(seed: int = 0, part: int = 0) -> dict:
    splits = jax.random.split(jax.random.key(seed), 8)
    part_keys = jax.random.split(jax.random.fold_in(splits[7], part), 8)
    learner_weight = draw_learner_weight(jax.random.fold_in(jax.random.fold_in(splits[7], part), 71), part)
    hidden_states = scatter_about(part_keys[1], (STEPS, ROWS, D), 1.0, 6.0, ((1, 4),))
    queries = draw_queries(jax.random.fold_in(jax.random.fold_in(splits[7], part), 71), part)
    cache_keys = draw_cache_keys(jax.random.fold_in(jax.random.fold_in(splits[7], part), 71), part)
    cache_values = scatter_about(part_keys[4], (SLOTS, BLOCK, KVH * HD), 1.0, 6.0, ((0, 4), (2, 4)))
    block_table = draw_block_table(jax.random.fold_in(jax.random.fold_in(splits[7], part), 71), part)
    lengths = draw_lengths(jax.random.fold_in(jax.random.fold_in(splits[7], part), 71), part)
    return dict(learner_weight=learner_weight, hidden_states=hidden_states, queries=queries, cache_keys=cache_keys, cache_values=cache_values, block_table=block_table, lengths=lengths)


EPSILON = 1e-06

def reference(learner_weight, hidden_states, queries, cache_keys, cache_values, block_table, lengths):
    grouped = learner_weight.astype(jnp.float32).reshape(D, 2 * KVH, HD)
    highest = lax.optimization_barrier(jnp.max(grouped, axis=2, keepdims=True))
    lowest = lax.optimization_barrier(jnp.min(grouped, axis=2, keepdims=True))
    middle = 0.5 * (highest + lowest)
    spread = 0.5 * (highest - lowest) + EPSILON
    ratio = (grouped - middle) / spread
    codes = jnp.floor(jnp.clip(ratio, -1.0, 1.0) * 7.5 + 8.0)
    payload = lax.optimization_barrier(codes.astype(jnp.bfloat16))
    synced = ((payload.astype(jnp.float32) - 7.5) / 7.5 * spread + middle).astype(jnp.bfloat16).reshape(D, 2 * KVH * HD)
    projected = jnp.dot(hidden_states.reshape(STEPS * ROWS, D), synced, preferred_element_type=jnp.float32)
    new_entries = lax.optimization_barrier(projected.astype(jnp.bfloat16).reshape(STEPS, ROWS, 2 * KVH * HD))
    fresh = new_entries.reshape(STEPS, ROWS, KVH, 2, HD).astype(jnp.float32)
    replica = jnp.arange(ROWS, dtype=jnp.int32) // ROWS_DEV
    slots = (block_table + (replica * POOL)[:, None]).astype(jnp.int32)
    factor = 1.0 / math.sqrt(HD)
    group_size = QH // KVH
    span = MAXB * BLOCK

    def one_row(index):
        keys = cache_keys[slots[index]].reshape(span, KVH, HD).astype(jnp.float32)
        values = cache_values[slots[index]].reshape(span, KVH, HD).astype(jnp.float32)
        query = queries[:, index].reshape(STEPS, KVH, group_size, HD).astype(jnp.float32)
        fresh_keys = fresh[:, index, :, 0]
        fresh_values = fresh[:, index, :, 1]
        cached = jnp.einsum('skgd,lkd->skgl', query, keys) * factor
        recent = jnp.einsum('skgd,tkd->skgt', query, fresh_keys) * factor
        visible = jnp.arange(span, dtype=jnp.int32) < lengths[index]
        cached = jnp.where(visible[None, None, None, :], cached, -jnp.inf)
        order = jnp.arange(STEPS, dtype=jnp.int32)
        causal = order[None, :] <= order[:, None]
        recent = jnp.where(causal[:, None, None, :], recent, -jnp.inf)
        peak = jnp.maximum(lax.optimization_barrier(jnp.max(cached, axis=-1, keepdims=True)), lax.optimization_barrier(jnp.max(recent, axis=-1, keepdims=True)))
        cached_weight = jnp.exp(cached - peak)
        recent_weight = jnp.exp(recent - peak)
        total = lax.optimization_barrier(jnp.sum(cached_weight, axis=-1)) + lax.optimization_barrier(jnp.sum(recent_weight, axis=-1))
        cached_round = lax.optimization_barrier(cached_weight.astype(jnp.bfloat16)).astype(jnp.float32)
        recent_round = lax.optimization_barrier(recent_weight.astype(jnp.bfloat16)).astype(jnp.float32)
        mixed = jnp.einsum('skgl,lkd->skgd', cached_round, values) + jnp.einsum('skgt,tkd->skgd', recent_round, fresh_values)
        return (mixed / total[..., None]).astype(jnp.bfloat16).reshape(STEPS, QH * HD)
    attended = lax.map(one_row, jnp.arange(ROWS, dtype=jnp.int32))
    return (new_entries, jnp.swapaxes(attended, 0, 1))
```

```python
import functools
import math

import jax
import jax.numpy as jnp
from jax import lax
from jax.experimental import pallas as pl
from jax.experimental.pallas import tpu as pltpu
from jax.sharding import PartitionSpec as P

KVH = 8
HD = 128
EPSILON = 1e-06
LANES_LAST = (((1,), (1,)), ((), ()))


def in_vmem():
    return pl.BlockSpec(memory_space=pltpu.VMEM)


def in_smem():
    return pl.BlockSpec(memory_space=pltpu.SMEM)


def quantize_kernel(weight, synced):
    rows, width = weight.shape
    chunk = min(rows, 32)

    def step(index, carry):
        at = pl.ds(pl.multiple_of(index * chunk, chunk), chunk)
        for group in range(width // HD):
            columns = slice(group * HD, (group + 1) * HD)
            entries = weight[at, columns].astype(jnp.float32)
            highest = jnp.max(entries, axis=1, keepdims=True)
            lowest = jnp.min(entries, axis=1, keepdims=True)
            middle = 0.5 * (highest + lowest)
            spread = 0.5 * (highest - lowest) + EPSILON
            levels = (entries - middle) * (7.5 / spread)
            codes = jnp.floor(jnp.clip(levels, -7.5, 7.5) + 8.0)
            restored = (codes - 7.5) * (spread * (1 / 7.5)) + middle
            synced[at, columns] = restored.astype(jnp.bfloat16)
        return carry

    lax.fori_loop(0, rows // chunk, step, 0)


def quantize(weight):
    return pl.pallas_call(
        quantize_kernel,
        out_shape=jax.ShapeDtypeStruct(weight.shape, jnp.bfloat16),
        in_specs=[in_vmem()],
        out_specs=in_vmem(),
        name="quantize",
    )(weight)


def project_kernel(tokens, places, synced, *refs):
    states, out = refs[:-1], refs[-1]
    across, width = out.shape[1], out.shape[3]
    stacked = jnp.concatenate([block[...] for block in states], axis=0)
    for column in range(across):
        part = jnp.dot(
            stacked,
            synced[:, column * width : (column + 1) * width],
            preferred_element_type=jnp.float32,
        ).astype(jnp.bfloat16)
        for index in range(len(states)):
            out[places[index], column] = part[index * tokens : (index + 1) * tokens]


def project(places, synced, states, across):
    tokens = states[0].shape[0]
    width = synced.shape[1] // across
    return pl.pallas_call(
        functools.partial(project_kernel, tokens),
        out_shape=jax.ShapeDtypeStruct((len(states), across, tokens, width), jnp.bfloat16),
        in_specs=[in_smem(), in_vmem()] + [in_vmem()] * len(states),
        out_specs=in_vmem(),
        name="project",
    )(places, synced, *states)


def cached_kernel(steps, table, lengths, query, keys, values, mixed, peaks, totals, wide):
    tokens, width = query.shape
    rows = tokens // steps
    heads = keys.shape[2] // HD
    group = width // (heads * HD)
    block = keys.shape[1]
    blocks = table.shape[1]
    factor = 1.0 / math.sqrt(HD)
    for member in range(heads * group):
        lanes = slice(member * HD, (member + 1) * HD)
        wide[member * tokens : (member + 1) * tokens] = query[:, lanes].astype(jnp.float32)
    for row in range(rows):
        length = lengths[row]
        for head in range(heads):
            lanes = slice(head * HD, (head + 1) * HD)
            at = pl.ds(head * group * tokens + row, group * steps, stride=rows)
            stacked = wide[at, :].astype(jnp.bfloat16)
            scores = []
            for part in range(blocks):
                score = lax.dot_general(
                    stacked,
                    keys[table[row, part], :, lanes],
                    LANES_LAST,
                    preferred_element_type=jnp.float32,
                )
                position = lax.broadcasted_iota(jnp.int32, (1, block), 1) + part * block
                scores.append(jnp.where(position < length, score * factor, -jnp.inf))
            peak = functools.reduce(
                jnp.maximum, [jnp.max(score, axis=1, keepdims=True) for score in scores]
            )
            total = jnp.zeros_like(peak)
            mix = jnp.zeros((steps * group, HD), jnp.float32)
            for part in range(blocks):
                weight = jnp.exp(scores[part] - peak)
                total = total + jnp.sum(weight, axis=1, keepdims=True)
                mix = mix + jnp.dot(
                    weight.astype(jnp.bfloat16),
                    values[table[row, part], :, lanes],
                    preferred_element_type=jnp.float32,
                )
            mixed[at, :] = mix
            peaks[at, :] = jnp.broadcast_to(peak, mix.shape)
            totals[at, :] = jnp.broadcast_to(total, mix.shape)


def cached(table, lengths, query, keys, values, steps):
    shape = (query.size // HD, HD)
    result = jax.ShapeDtypeStruct(shape, jnp.float32)
    return pl.pallas_call(
        functools.partial(cached_kernel, steps),
        out_shape=(result, result, result),
        in_specs=[in_smem(), in_smem(), in_vmem(), in_vmem(), in_vmem()],
        out_specs=(in_vmem(), in_vmem(), in_vmem()),
        scratch_shapes=[pltpu.VMEM(shape, jnp.float32)],
        name="cached",
    )(table, lengths, query, keys, values)


def finish_kernel(steps, parts, query, mixed, peaks, totals, fresh, attended):
    tokens, width = query.shape
    rows = tokens // steps
    heads = fresh.shape[1] // (2 * HD)
    group = width // (heads * HD)
    factor = 1.0 / math.sqrt(HD)
    total = parts[0].astype(jnp.float32)
    for index in range(1, parts.shape[0]):
        total = total + parts[index].astype(jnp.float32)
    entries = total.astype(jnp.bfloat16)
    fresh[...] = entries
    shape = (group * tokens, tokens)
    asking = lax.broadcasted_iota(jnp.int32, shape, 0) % tokens
    told = lax.broadcasted_iota(jnp.int32, shape, 1)
    allowed = (asking % rows == told % rows) & (told <= asking)
    for head in range(heads):
        key = entries[:, 2 * head * HD : (2 * head + 1) * HD]
        value = entries[:, (2 * head + 1) * HD : (2 * head + 2) * HD]
        places = [
            slice((head * group + member) * HD, (head * group + member + 1) * HD)
            for member in range(group)
        ]
        stacked = jnp.concatenate([query[:, place] for place in places], axis=0)
        score = lax.dot_general(stacked, key, LANES_LAST, preferred_element_type=jnp.float32)
        score = jnp.where(allowed, score * factor, -jnp.inf)
        at = slice(head * group * tokens, (head + 1) * group * tokens)
        before = peaks[at]
        peak = jnp.maximum(before, jnp.max(score, axis=1, keepdims=True))
        weight = jnp.exp(score - peak[:, :tokens])
        shrink = jnp.exp(before - peak)
        mix = mixed[at] * shrink + jnp.dot(
            weight.astype(jnp.bfloat16), value, preferred_element_type=jnp.float32
        )
        sums = totals[at] * shrink + jnp.sum(weight, axis=1, keepdims=True)
        result = (mix / sums).astype(jnp.bfloat16)
        for member, place in enumerate(places):
            attended[:, place] = result[member * tokens : (member + 1) * tokens]


def finish(parts, query, mixed, peaks, totals, steps):
    return pl.pallas_call(
        functools.partial(finish_kernel, steps),
        out_shape=(
            jax.ShapeDtypeStruct(parts.shape[1:], jnp.bfloat16),
            jax.ShapeDtypeStruct(query.shape, jnp.bfloat16),
        ),
        in_specs=[in_vmem()] * 5,
        out_specs=(in_vmem(), in_vmem()),
        name="finish",
    )(parts, query, mixed, peaks, totals)


def body(learner_weight, hidden_states, queries, cache_keys, cache_values, block_table, lengths):
    steps, rows, model_width = hidden_states.shape
    tokens = steps * rows
    shard_rows = learner_weight.shape[0]
    replicas, across = lax.axis_size("fsdp"), lax.axis_size("tp")
    replica, column = lax.axis_index("fsdp"), lax.axis_index("tp")
    flat_states = hidden_states.reshape(tokens, model_width)
    query = queries.reshape(tokens, queries.shape[2])
    places = replica ^ jnp.arange(replicas, dtype=jnp.int32)
    states = []
    for hop in range(replicas):
        start = ((replica ^ hop) * across + column) * shard_rows
        block = lax.dynamic_slice(flat_states, (0, start), (tokens, shard_rows))
        if hop:
            block = lax.ppermute(block, "fsdp", [(i, i ^ hop) for i in range(replicas)])
        states.append(block)
    synced = quantize(learner_weight)
    parts = project(places, synced, states, across)
    parts = parts.reshape((replicas * across,) + parts.shape[2:])
    parts = lax.all_to_all(parts, ("fsdp", "tp"), 0, 0, tiled=True)
    mixed, peaks, totals = cached(block_table, lengths, query, cache_keys, cache_values, steps)
    fresh, attended = finish(parts, query, mixed, peaks, totals, steps)
    return (fresh.reshape(steps, rows, fresh.shape[1]), attended.reshape(queries.shape))


def solution(mesh):
    return jax.shard_map(
        body,
        mesh=mesh,
        in_specs=(
            P(("groups", "fsdp", "tp"), None),
            P("groups", "fsdp", None),
            P("groups", "fsdp", "tp"),
            P(("groups", "fsdp"), None, "tp"),
            P(("groups", "fsdp"), None, "tp"),
            P(("groups", "fsdp"), None),
            P(("groups", "fsdp")),
        ),
        out_specs=(P("groups", "fsdp", "tp"), P("groups", "fsdp", "tp")),
        check_vma=False,
    )
```

```python
import functools
import math

import jax
import jax.numpy as jnp
from jax import lax
from jax.experimental import pallas as pl
from jax.experimental.pallas import tpu as pltpu
from jax.sharding import PartitionSpec as P

KVH = 8
HD = 128
EPSILON = 1e-06
PIECE = 256
GRANT = pltpu.CompilerParams(vmem_limit_bytes=16 * 1024 * 1024)
LANES_LAST = (((1,), (1,)), ((), ()))


def in_vmem():
    return pl.BlockSpec(memory_space=pltpu.VMEM)


def in_smem():
    return pl.BlockSpec(memory_space=pltpu.SMEM)


def as_rows(block):
    return block.astype(jnp.float32).reshape(-1, block.shape[-1]).astype(block.dtype)


def collect_kernel(pairs, weight, states, *refs):
    done, given, blocks = refs[-1], refs[:pairs], refs[pairs:-1]
    rows, block = given[0].shape
    replica, column = lax.axis_index("fsdp"), lax.axis_index("tp")
    across = 2 * pairs

    def lanes(start, size):
        return pl.ds(pl.multiple_of(start * size, HD), size)

    copies = []
    for hop, target in enumerate(blocks):
        owner = (replica ^ hop) * across
        for half, holder in enumerate((column, column ^ 1)):
            copies.append(
                (
                    states.at[:, :, lanes(owner + holder, rows)],
                    target.at[:, :, half * rows : (half + 1) * rows],
                )
            )
    for pair, target in enumerate(given):
        copies.append((weight.at[:, lanes(2 * pair + 1 - column % 2, block)], target))
    copies = [
        pltpu.make_async_copy(source, target, done.at[index])
        for index, (source, target) in enumerate(copies)
    ]
    for copy in copies:
        copy.start()
    for copy in copies:
        copy.wait()


def collect(weight, states, replicas, pairs):
    rows, width = weight.shape
    steps, tokens, _ = states.shape
    block = width // (2 * pairs)
    given = jax.ShapeDtypeStruct((rows, block), weight.dtype)
    state = jax.ShapeDtypeStruct((steps, tokens, 2 * rows), states.dtype)
    results = pl.pallas_call(
        functools.partial(collect_kernel, pairs),
        out_shape=(given,) * pairs + (state,) * replicas,
        in_specs=[pl.BlockSpec(memory_space=pltpu.HBM)] * 2,
        out_specs=(in_vmem(),) * (pairs + replicas),
        scratch_shapes=[pltpu.SemaphoreType.DMA((pairs + 2 * replicas,))],
        compiler_params=GRANT,
        name="collect",
    )(*[pltpu.with_memory_space_constraint(array, pltpu.HBM) for array in (weight, states)])
    return results[:pairs], results[pairs:]


def collect_narrow(weight, states, replicas, pairs):
    rows, width = weight.shape
    steps, tokens, _ = states.shape
    block = width // (2 * pairs)
    replica, column = lax.axis_index("fsdp"), lax.axis_index("tp")
    given = [
        lax.dynamic_slice(weight, (0, (2 * pair + 1 - column % 2) * block), (rows, block))
        for pair in range(pairs)
    ]
    blocks = []
    for hop in range(replicas):
        owner = (replica ^ hop) * 2 * pairs
        halves = [
            lax.dynamic_slice(states, (0, 0, (owner + holder) * rows), (steps, tokens, rows))
            for holder in (column, column ^ 1)
        ]
        blocks.append(jnp.concatenate(halves, axis=2))
    return given, blocks


def quantize_kernel(block, *refs):
    weights, synced = refs[:-1], refs[-1]
    kept = synced.shape[0]
    width = min(PIECE, block)
    parity = lax.axis_index("tp") % 2
    across = lax.broadcasted_iota(jnp.int32, (width, width), 0)
    along = lax.broadcasted_iota(jnp.int32, (width, width), 1)
    identity = jnp.where(across == along, 1.0, 0.0).astype(jnp.bfloat16)
    for start in range(0, kept, width):
        pair, offset = start // block, start % block
        if len(weights) > 1:
            entries = weights[pair][:, offset : offset + width]
        else:
            at = (2 * pair + parity) * block + offset
            entries = weights[0][:, pl.ds(pl.multiple_of(at, width), width)]
        turned = lax.dot_general(identity, entries, LANES_LAST, preferred_element_type=jnp.float32)
        for offset in range(0, width, HD):
            entries = turned[offset : offset + HD]
            highest = jnp.max(entries, axis=0, keepdims=True)
            lowest = jnp.min(entries, axis=0, keepdims=True)
            middle = 0.5 * (highest + lowest)
            spread = 0.5 * (highest - lowest) + EPSILON
            levels = (entries - middle) * (7.5 / spread)
            codes = jnp.floor(jnp.clip(levels, -7.5, 7.5) + 8.0)
            restored = (codes - 7.5) * (spread * (1 / 7.5)) + middle
            synced[start + offset : start + offset + HD] = restored.astype(jnp.bfloat16)


def quantize(block, weights, kept):
    return pl.pallas_call(
        functools.partial(quantize_kernel, block),
        out_shape=jax.ShapeDtypeStruct((kept, weights[0].shape[0]), jnp.bfloat16),
        in_specs=[in_vmem()] * len(weights),
        out_specs=in_vmem(),
        compiler_params=GRANT,
        name="quantize",
    )(*weights)


def project_kernel(replicas, mine, theirs, *refs):
    states, outs = refs[:replicas], refs[replicas:]
    tokens, width = outs[0].shape[1:]
    rows = mine.shape[1]
    pair = lax.axis_index("tp") // 2
    stacked = jnp.concatenate([as_rows(block[...]) for block in states], axis=0)
    for distance, out in reversed(list(enumerate(outs))):
        at = pl.ds(pl.multiple_of((pair ^ distance) * width, width), width)
        part = lax.dot_general(
            stacked[:, :rows], mine[at, :], LANES_LAST, preferred_element_type=jnp.float32
        ) + lax.dot_general(
            stacked[:, rows:], theirs[at, :], LANES_LAST, preferred_element_type=jnp.float32
        )
        out[...] = part.astype(jnp.bfloat16).reshape(out.shape)


def project(mine, theirs, states, pairs):
    tokens = states[0].shape[0] * states[0].shape[1]
    width = mine.shape[0] // pairs
    shape = jax.ShapeDtypeStruct((len(states), tokens, width), jnp.bfloat16)
    return pl.pallas_call(
        functools.partial(project_kernel, len(states)),
        out_shape=(shape,) * pairs,
        in_specs=[in_vmem()] * (2 + len(states)),
        out_specs=(in_vmem(),) * pairs,
        compiler_params=GRANT,
        name="project",
    )(mine, theirs, *states)


def cached_kernel(first, last, table, lengths, query, keys, values, *refs):
    asked, mixed, peaks, totals, wide = refs[-5:]
    steps, rows, width = query.shape
    tokens = steps * rows
    heads = keys.shape[2] // HD
    group = width // (heads * HD)
    block = keys.shape[1]
    blocks = table.shape[1]
    factor = 1.0 / math.sqrt(HD)
    for member in range(heads * group):
        lanes = slice(member * HD, (member + 1) * HD)
        every = query[:, :, lanes].astype(jnp.float32).reshape(tokens, HD)
        wide[member * tokens : (member + 1) * tokens] = every
        if not first:
            asked[member * tokens : (member + 1) * tokens] = every.astype(jnp.bfloat16)
    for row in range(first, last):
        length = lengths[row]
        for head in range(heads):
            lanes = slice(head * HD, (head + 1) * HD)
            at = pl.ds(head * group * tokens + row, group * steps, stride=rows)
            stacked = wide[at, :].astype(jnp.bfloat16)
            scores = []
            for part in range(blocks):
                score = lax.dot_general(
                    stacked,
                    keys[table[row, part], :, lanes],
                    LANES_LAST,
                    preferred_element_type=jnp.float32,
                )
                position = lax.broadcasted_iota(jnp.int32, (1, block), 1) + part * block
                scores.append(jnp.where(position < length, score * factor, -jnp.inf))
            peak = functools.reduce(
                jnp.maximum, [jnp.max(score, axis=1, keepdims=True) for score in scores]
            )
            total = jnp.zeros_like(peak)
            mix = jnp.zeros((steps * group, HD), jnp.float32)
            for part in range(blocks):
                weight = jnp.exp(scores[part] - peak)
                total = total + jnp.sum(weight, axis=1, keepdims=True)
                mix = mix + jnp.dot(
                    weight.astype(jnp.bfloat16),
                    values[table[row, part], :, lanes],
                    preferred_element_type=jnp.float32,
                )
            mixed[at, :] = mix
            peaks[at, :] = jnp.broadcast_to(peak, mix.shape)
            totals[at, :] = jnp.broadcast_to(total, mix.shape)


def cached(first, last, table, lengths, query, keys, values, before=()):
    shape = (query.size // HD, HD)
    result = jax.ShapeDtypeStruct(shape, jnp.float32)
    return pl.pallas_call(
        functools.partial(cached_kernel, first, last),
        out_shape=(jax.ShapeDtypeStruct(shape, jnp.bfloat16), result, result, result),
        in_specs=[in_smem()] * 2 + [in_vmem()] * (3 + len(before)),
        out_specs=(in_vmem(),) * 4,
        scratch_shapes=[pltpu.VMEM(shape, jnp.float32)],
        input_output_aliases={5 + index: index for index in range(len(before))},
        compiler_params=GRANT,
        name="cached",
    )(table, lengths, query, keys, values, *before)


def finish_kernel(kept, asked, mixed, peaks, totals, *refs):
    parts, (fresh, attended) = refs[:-2], refs[-2:]
    steps, rows, width = attended.shape
    tokens = steps * rows
    heads = fresh.shape[2] // (2 * HD)
    group = width // (heads * HD)
    factor = 1.0 / math.sqrt(HD)
    total = kept[...]
    for part in parts:
        total = total + part[...].astype(jnp.float32)
    entries = total.astype(jnp.bfloat16)
    fresh[...] = entries.astype(jnp.float32).reshape(fresh.shape).astype(jnp.bfloat16)
    shape = (group * tokens, tokens)
    asking = lax.broadcasted_iota(jnp.int32, shape, 0) % tokens
    told = lax.broadcasted_iota(jnp.int32, shape, 1)
    allowed = (asking % rows == told % rows) & (told <= asking)
    for head in range(heads):
        key = entries[:, 2 * head * HD : (2 * head + 1) * HD]
        value = entries[:, (2 * head + 1) * HD : (2 * head + 2) * HD]
        at = slice(head * group * tokens, (head + 1) * group * tokens)
        score = lax.dot_general(asked[at], key, LANES_LAST, preferred_element_type=jnp.float32)
        score = jnp.where(allowed, score * factor, -jnp.inf)
        before = peaks[at]
        peak = jnp.maximum(before, jnp.max(score, axis=1, keepdims=True))
        weight = jnp.exp(score - peak[:, :tokens])
        shrink = jnp.exp(before - peak)
        mix = mixed[at] * shrink + jnp.dot(
            weight.astype(jnp.bfloat16), value, preferred_element_type=jnp.float32
        )
        sums = totals[at] * shrink + jnp.sum(weight, axis=1, keepdims=True)
        result = mix / sums
        for member in range(group):
            lanes = slice((head * group + member) * HD, (head * group + member + 1) * HD)
            some = result[member * tokens : (member + 1) * tokens]
            attended[:, :, lanes] = some.reshape(steps, rows, HD).astype(jnp.bfloat16)


def finish(kept, parts, asked, mixed, peaks, totals, shape):
    return pl.pallas_call(
        finish_kernel,
        out_shape=(
            jax.ShapeDtypeStruct(shape[:2] + kept.shape[1:], jnp.bfloat16),
            jax.ShapeDtypeStruct(shape, jnp.bfloat16),
        ),
        in_specs=[in_vmem()] * (5 + len(parts)),
        out_specs=(in_vmem(), in_vmem()),
        compiler_params=GRANT,
        name="finish",
    )(kept, asked, mixed, peaks, totals, *parts)


def body(learner_weight, hidden_states, queries, cache_keys, cache_values, block_table, lengths):
    steps, rows, model_width = hidden_states.shape
    shard_rows, width = learner_weight.shape
    replicas, across = lax.axis_size("fsdp"), lax.axis_size("tp")
    replica, column = lax.axis_index("fsdp"), lax.axis_index("tp")
    block = width // across
    pairs = across // 2

    def swap(array, axis, distance):
        count = lax.axis_size(axis)
        return lax.ppermute(array, axis, [(i, i ^ distance) for i in range(count)])

    gather = collect_narrow if shard_rows % HD else collect
    given, states = gather(learner_weight, hidden_states, replicas, pairs)
    taken = [swap(part, "tp", 1) for part in given]
    states = list(states)
    for hop in range(1, replicas):
        states[hop] = swap(states[hop], "fsdp", hop)
    mine = quantize(block, [learner_weight], width // 2)
    theirs = quantize(block, taken, width // 2)
    parts = list(project(mine, theirs, states, pairs))
    middle = rows // 2
    caches = (queries, cache_keys, cache_values)
    seen = cached(0, middle, block_table, lengths, *caches)
    while len(parts) > 1:
        half = len(parts) // 2
        moved = swap(jnp.stack(parts[half:]).astype(jnp.bfloat16), "tp", 2 * half)
        moved, lengths = lax.optimization_barrier((moved, lengths))
        parts = [
            part.astype(jnp.float32) + moved[index].astype(jnp.float32)
            for index, part in enumerate(parts[:half])
        ]
    sums = parts[0]
    arrived = [swap(sums[hop].astype(jnp.bfloat16), "fsdp", hop) for hop in range(1, replicas)]
    asked, mixed, peaks, totals = cached(middle, rows, block_table, lengths, *caches, before=seen)
    return finish(sums[0], arrived, asked, mixed, peaks, totals, queries.shape)


def solution(mesh):
    return jax.shard_map(
        body,
        mesh=mesh,
        in_specs=(
            P(("groups", "fsdp", "tp"), None),
            P("groups", "fsdp", None),
            P("groups", "fsdp", "tp"),
            P(("groups", "fsdp"), None, "tp"),
            P(("groups", "fsdp"), None, "tp"),
            P(("groups", "fsdp"), None),
            P(("groups", "fsdp")),
        ),
        out_specs=(P("groups", "fsdp", "tp"), P("groups", "fsdp", "tp")),
        check_vma=False,
    )
```

```python
import functools
import math

import jax
import jax.numpy as jnp
from jax import lax
from jax.experimental import pallas as pl
from jax.experimental.pallas import tpu as pltpu
from jax.sharding import PartitionSpec as P

KVH = 8
HD = 128
EPSILON = 1e-06
PIECE = 256
SENDING = (2, 3, 1)
RETURNING = (3, 2, 1)
GRANT = pltpu.CompilerParams(vmem_limit_bytes=16 * 1024 * 1024)
LANES_LAST = (((1,), (1,)), ((), ()))


def in_vmem():
    return pl.BlockSpec(memory_space=pltpu.VMEM)


def in_smem():
    return pl.BlockSpec(memory_space=pltpu.SMEM)


def in_hbm(array):
    return pltpu.with_memory_space_constraint(array, pltpu.HBM)


def as_rows(block):
    return block.astype(jnp.float32).reshape(-1, block.shape[-1]).astype(block.dtype)


def visits(count, first):
    return [hop for hop in first if hop < count] + [hop for hop in range(count) if hop not in first]


def collect_kernel(states, *refs):
    blocks, done = refs[:-1], refs[-1]
    rows = blocks[0].shape[2] // 2
    replica, column, across = lax.axis_index("fsdp"), lax.axis_index("tp"), lax.axis_size("tp")
    copies = []
    for hop, target in enumerate(blocks):
        for half, holder in enumerate((column, column ^ 1)):
            start = ((replica ^ hop) * across + holder) * rows
            source = states.at[:, :, pl.ds(pl.multiple_of(start, HD), rows)]
            target_half = target.at[:, :, half * rows : (half + 1) * rows]
            copies.append(pltpu.make_async_copy(source, target_half, done.at[2 * hop + half]))
            copies[-1].start()
    for copy in copies:
        copy.wait()


def collect(states, rows, replicas):
    result = jax.ShapeDtypeStruct(states.shape[:2] + (2 * rows,), states.dtype)
    if rows % HD:
        replica, column, across = lax.axis_index("fsdp"), lax.axis_index("tp"), lax.axis_size("tp")
        blocks = []
        for hop in range(replicas):
            starts = [((replica ^ hop) * across + holder) * rows for holder in (column, column ^ 1)]
            shape = states.shape[:2] + (rows,)
            halves = [lax.dynamic_slice(states, (0, 0, start), shape) for start in starts]
            blocks.append(jnp.concatenate(halves, axis=2))
        return blocks
    return pl.pallas_call(
        collect_kernel,
        out_shape=(result,) * replicas,
        in_specs=[pl.BlockSpec(memory_space=pltpu.HBM)],
        out_specs=(in_vmem(),) * replicas,
        scratch_shapes=[pltpu.SemaphoreType.DMA((2 * replicas,))],
        compiler_params=GRANT,
        name="collect",
    )(in_hbm(states))


def restore(entries, identity):
    turned = lax.dot_general(identity, entries, LANES_LAST, preferred_element_type=jnp.float32)
    results = []
    for offset in range(0, turned.shape[0], HD):
        group = turned[offset : offset + HD]
        highest = jnp.max(group, axis=0, keepdims=True)
        lowest = jnp.min(group, axis=0, keepdims=True)
        middle = 0.5 * (highest + lowest)
        spread = 0.5 * (highest - lowest) + EPSILON
        scale = 7.5 / spread
        size = spread * (1 / 7.5)
        codes = jnp.floor(jnp.clip(group * scale + (8.0 - middle * scale), 0.5, 15.5))
        restored = codes * size + (middle - 7.5 * size)
        results.append(restored.astype(jnp.bfloat16))
    return results


def quantize_kernel(weight, taken, mine, theirs, held, done):
    pairs, rows, block = held.shape
    width = min(PIECE, block)
    parity = lax.axis_index("tp") % 2
    copies = {}
    for pair in range(pairs):
        for start in range(0, block, width):
            at = pl.ds(pl.multiple_of((2 * pair + parity) * block + start, HD), width)
            copies[pair, start] = pltpu.make_async_copy(
                weight.at[:, at],
                held.at[pair, :, start : start + width],
                done.at[pair, start // width],
            )
            copies[pair, start].start()
    across = lax.broadcasted_iota(jnp.int32, (width, width), 0)
    along = lax.broadcasted_iota(jnp.int32, (width, width), 1)
    identity = jnp.where(across == along, 1.0, 0.0).astype(jnp.bfloat16)
    for own, out in ((False, theirs), (True, mine)):
        for pair in range(pairs):
            for start in range(0, block, width):
                if own:
                    copies[pair, start].wait()
                    entries = held[pair, :, start : start + width]
                else:
                    at = (2 * pair + parity) * block + start
                    entries = taken[:, pl.ds(pl.multiple_of(at, HD), width)]
                for index, result in enumerate(restore(entries, identity)):
                    at = pair * block + start + index * HD
                    out[at : at + HD] = result


def quantize(weight, taken, pairs):
    rows, width = weight.shape
    block = width // (2 * pairs)
    result = jax.ShapeDtypeStruct((pairs * block, rows), jnp.bfloat16)
    return pl.pallas_call(
        quantize_kernel,
        out_shape=(result, result),
        in_specs=[pl.BlockSpec(memory_space=pltpu.HBM), in_vmem()],
        out_specs=(in_vmem(), in_vmem()),
        scratch_shapes=[
            pltpu.VMEM((pairs, rows, block), weight.dtype),
            pltpu.SemaphoreType.DMA((pairs, pl.cdiv(block, PIECE))),
        ],
        compiler_params=GRANT,
        name="quantize",
    )(in_hbm(weight), taken)


def project_kernel(order, mine, theirs, *refs):
    replicas = len(order)
    states, outs = refs[:replicas], refs[replicas:]
    tokens, width = outs[0].shape[1:]
    rows = mine.shape[1]
    pair = lax.axis_index("tp") // 2
    stacked = [as_rows(states[order.index(hop)][...]) for hop in range(replicas)]
    stacked = jnp.concatenate(stacked, axis=0)
    for distance, out in reversed(list(enumerate(outs))):
        at = pl.ds(pl.multiple_of((pair ^ distance) * width, width), width)
        part = lax.dot_general(
            stacked[:, :rows], mine[at, :], LANES_LAST, preferred_element_type=jnp.float32
        ) + lax.dot_general(
            stacked[:, rows:], theirs[at, :], LANES_LAST, preferred_element_type=jnp.float32
        )
        out[...] = part.astype(jnp.bfloat16).reshape(out.shape)


def project(mine, theirs, states, pairs):
    order = visits(len(states), SENDING)
    tokens = states[0].shape[0] * states[0].shape[1]
    width = mine.shape[0] // pairs
    shape = jax.ShapeDtypeStruct((len(states), tokens, width), jnp.bfloat16)
    return pl.pallas_call(
        functools.partial(project_kernel, order),
        out_shape=(shape,) * pairs,
        in_specs=[in_vmem()] * (2 + len(states)),
        out_specs=(in_vmem(),) * pairs,
        compiler_params=GRANT,
        name="project",
    )(mine, theirs, *[states[hop] for hop in order])


def weigh_kernel(table, lengths, query, keys, asked, weights, peaks, totals, wide):
    steps, rows, width = query.shape
    tokens = steps * rows
    heads = keys.shape[2] // HD
    group = width // (heads * HD)
    block = keys.shape[1]
    blocks = table.shape[1]
    factor = 1.0 / math.sqrt(HD)
    for member in range(heads * group):
        lanes = slice(member * HD, (member + 1) * HD)
        every = query[:, :, lanes].astype(jnp.float32).reshape(tokens, HD)
        wide[member * tokens : (member + 1) * tokens] = every
        asked[member * tokens : (member + 1) * tokens] = every.astype(jnp.bfloat16)
    for row in range(rows):
        length = lengths[row]
        for head in range(heads):
            lanes = slice(head * HD, (head + 1) * HD)
            at = pl.ds(head * group * tokens + row, group * steps, stride=rows)
            stacked = wide[at, :].astype(jnp.bfloat16)
            scores = []
            for part in range(blocks):
                score = lax.dot_general(
                    stacked,
                    keys[table[row, part], :, lanes],
                    LANES_LAST,
                    preferred_element_type=jnp.float32,
                )
                position = lax.broadcasted_iota(jnp.int32, (1, block), 1) + part * block
                scores.append(jnp.where(position < length, score * factor, -jnp.inf))
            peak = functools.reduce(
                jnp.maximum, [jnp.max(score, axis=1, keepdims=True) for score in scores]
            )
            total = jnp.zeros_like(peak)
            for part in range(blocks):
                weight = jnp.exp(scores[part] - peak)
                total = total + jnp.sum(weight, axis=1, keepdims=True)
                weights[row * heads + head, :, part * block : (part + 1) * block] = weight.astype(
                    jnp.bfloat16
                )
            peaks[at, :] = jnp.broadcast_to(peak, (group * steps, HD))
            totals[at, :] = jnp.broadcast_to(total, (group * steps, HD))


def weigh(table, lengths, query, keys):
    steps, rows, width = query.shape
    heads = keys.shape[2] // HD
    shape = (query.size // HD, HD)
    result = jax.ShapeDtypeStruct(shape, jnp.float32)
    span = table.shape[1] * keys.shape[1]
    weights = (rows * heads, steps * width // (heads * HD), span)
    return pl.pallas_call(
        weigh_kernel,
        out_shape=(
            jax.ShapeDtypeStruct(shape, jnp.bfloat16),
            jax.ShapeDtypeStruct(weights, jnp.bfloat16),
            result,
            result,
        ),
        in_specs=[in_smem()] * 2 + [in_vmem()] * 2,
        out_specs=(in_vmem(),) * 4,
        scratch_shapes=[pltpu.VMEM(shape, jnp.float32)],
        compiler_params=GRANT,
        name="weigh",
    )(table, lengths, query, keys)


def mix_kernel(table, weights, values, mixed):
    rows, blocks = table.shape
    block = values.shape[1]
    heads = values.shape[2] // HD
    asking = weights.shape[1]
    for row in range(rows):
        for head in range(heads):
            mix = jnp.zeros((asking, HD), jnp.float32)
            for part in range(blocks):
                mix = mix + jnp.dot(
                    weights[row * heads + head, :, part * block : (part + 1) * block],
                    values[table[row, part], :, head * HD : (head + 1) * HD],
                    preferred_element_type=jnp.float32,
                )
            mixed[pl.ds(head * asking * rows + row, asking, stride=rows), :] = mix


def mix(table, weights, values):
    shape = (weights.shape[0] * weights.shape[1], HD)
    return pl.pallas_call(
        mix_kernel,
        out_shape=jax.ShapeDtypeStruct(shape, jnp.float32),
        in_specs=[in_smem()] + [in_vmem()] * 2,
        out_specs=in_vmem(),
        compiler_params=GRANT,
        name="mix",
    )(table, weights, values)


def finish_kernel(kept, asked, mixed, peaks, totals, *refs):
    parts, (fresh, attended) = refs[:-2], refs[-2:]
    steps, rows, width = attended.shape
    tokens = steps * rows
    heads = fresh.shape[2] // (2 * HD)
    group = width // (heads * HD)
    factor = 1.0 / math.sqrt(HD)
    total = kept[...]
    for part in parts:
        total = total + part[...].astype(jnp.float32)
    entries = total.astype(jnp.bfloat16)
    fresh[...] = entries.astype(jnp.float32).reshape(fresh.shape).astype(jnp.bfloat16)
    shape = (group * tokens, tokens)
    asking = lax.broadcasted_iota(jnp.int32, shape, 0) % tokens
    told = lax.broadcasted_iota(jnp.int32, shape, 1)
    allowed = (asking % rows == told % rows) & (told <= asking)
    for head in range(heads):
        key = entries[:, 2 * head * HD : (2 * head + 1) * HD]
        value = entries[:, (2 * head + 1) * HD : (2 * head + 2) * HD]
        at = slice(head * group * tokens, (head + 1) * group * tokens)
        score = lax.dot_general(asked[at], key, LANES_LAST, preferred_element_type=jnp.float32)
        score = jnp.where(allowed, score * factor, -jnp.inf)
        before = peaks[at]
        peak = jnp.maximum(before, jnp.max(score, axis=1, keepdims=True))
        weight = jnp.exp(score - peak[:, :tokens])
        shrink = jnp.exp(before - peak)
        mix = mixed[at] * shrink + jnp.dot(
            weight.astype(jnp.bfloat16), value, preferred_element_type=jnp.float32
        )
        sums = totals[at] * shrink + jnp.sum(weight, axis=1, keepdims=True)
        result = mix / sums
        for member in range(group):
            lanes = slice((head * group + member) * HD, (head * group + member + 1) * HD)
            some = result[member * tokens : (member + 1) * tokens]
            attended[:, :, lanes] = some.reshape(steps, rows, HD).astype(jnp.bfloat16)


def finish(kept, parts, asked, mixed, peaks, totals, shape):
    return pl.pallas_call(
        finish_kernel,
        out_shape=(
            jax.ShapeDtypeStruct(shape[:2] + kept.shape[1:], jnp.bfloat16),
            jax.ShapeDtypeStruct(shape, jnp.bfloat16),
        ),
        in_specs=[in_vmem()] * (5 + len(parts)),
        out_specs=(in_vmem(), in_vmem()),
        compiler_params=GRANT,
        name="finish",
    )(kept, asked, mixed, peaks, totals, *parts)


def body(learner_weight, hidden_states, queries, cache_keys, cache_values, block_table, lengths):
    shard_rows = learner_weight.shape[0]
    replicas, across = lax.axis_size("fsdp"), lax.axis_size("tp")
    pairs = across // 2

    def swap(array, axis, distance):
        count = lax.axis_size(axis)
        return lax.ppermute(array, axis, [(i, i ^ distance) for i in range(count)])

    taken = swap(learner_weight, "tp", 1)
    states = list(collect(hidden_states, shard_rows, replicas))
    for hop in range(1, replicas):
        states[hop] = swap(states[hop], "fsdp", hop)
    mine, theirs = quantize(learner_weight, taken, pairs)
    parts = list(project(mine, theirs, states, pairs))
    asked, weights, peaks, totals = weigh(block_table, lengths, queries, cache_keys)
    while len(parts) > 1:
        half = len(parts) // 2
        moved = swap(jnp.stack(parts[half:]).astype(jnp.bfloat16), "tp", 2 * half)
        moved, block_table = lax.optimization_barrier((moved, block_table))
        parts = [
            part.astype(jnp.float32) + moved[index].astype(jnp.float32)
            for index, part in enumerate(parts[:half])
        ]
    sums = parts[0]
    arrived = [
        swap(sums[hop].astype(jnp.bfloat16), "fsdp", hop)
        for hop in visits(replicas, RETURNING)
        if hop
    ]
    mixed = mix(block_table, weights, cache_values)
    return finish(sums[0], arrived, asked, mixed, peaks, totals, queries.shape)


def solution(mesh):
    return jax.shard_map(
        body,
        mesh=mesh,
        in_specs=(
            P(("groups", "fsdp", "tp"), None),
            P("groups", "fsdp", None),
            P("groups", "fsdp", "tp"),
            P(("groups", "fsdp"), None, "tp"),
            P(("groups", "fsdp"), None, "tp"),
            P(("groups", "fsdp"), None),
            P(("groups", "fsdp")),
        ),
        out_specs=(P("groups", "fsdp", "tp"), P("groups", "fsdp", "tp")),
        check_vma=False,
    )
```

```python
import functools
import math

import jax
import jax.numpy as jnp
from jax import lax
from jax.experimental import pallas as pl
from jax.experimental.pallas import tpu as pltpu
from jax.sharding import PartitionSpec as P

KVH = 8
HD = 128
EPSILON = 1e-06
PIECE = 256
SENDING = (2, 3, 1)
RETURNING = (3, 2, 1)
GRANT = pltpu.CompilerParams(vmem_limit_bytes=16 * 1024 * 1024)
LANES_LAST = (((1,), (1,)), ((), ()))


def in_vmem():
    return pl.BlockSpec(memory_space=pltpu.VMEM)


def in_smem():
    return pl.BlockSpec(memory_space=pltpu.SMEM)


def in_hbm(array):
    return pltpu.with_memory_space_constraint(array, pltpu.HBM)


def as_rows(block):
    return block.astype(jnp.float32).reshape(-1, block.shape[-1]).astype(block.dtype)


def visits(count, first):
    return [hop for hop in first if hop < count] + [hop for hop in range(count) if hop not in first]


def collect_kernel(states, *refs):
    blocks, done = refs[:-1], refs[-1]
    width = blocks[0].shape[2]
    replica, pair, pairs = lax.axis_index("fsdp"), lax.axis_index("tp") // 2, lax.axis_size("tp") // 2
    copies = []
    for hop, target in enumerate(blocks):
        start = pl.multiple_of(((replica ^ hop) * pairs + pair) * width, HD)
        source = states.at[:, :, pl.ds(start, width)]
        copies.append(pltpu.make_async_copy(source, target, done.at[hop]))
    for copy in copies[1:] + copies[:1]:
        copy.start()
    for copy in copies:
        copy.wait()


def collect(states, width, replicas):
    shape = states.shape[:2] + (width,)
    if width % HD:
        replica, pair, pairs = (
            lax.axis_index("fsdp"),
            lax.axis_index("tp") // 2,
            lax.axis_size("tp") // 2,
        )
        starts = [((replica ^ hop) * pairs + pair) * width for hop in range(replicas)]
        return [lax.dynamic_slice(states, (0, 0, start), shape) for start in starts]
    return pl.pallas_call(
        collect_kernel,
        out_shape=(jax.ShapeDtypeStruct(shape, states.dtype),) * replicas,
        in_specs=[pl.BlockSpec(memory_space=pltpu.HBM)],
        out_specs=(in_vmem(),) * replicas,
        scratch_shapes=[pltpu.SemaphoreType.DMA((replicas,))],
        compiler_params=GRANT,
        name="collect",
    )(in_hbm(states))


def restore(entries, identity):
    turned = lax.dot_general(identity, entries, LANES_LAST, preferred_element_type=jnp.float32)
    results = []
    for offset in range(0, turned.shape[0], HD):
        group = turned[offset : offset + HD]
        highest = jnp.max(group, axis=0, keepdims=True)
        lowest = jnp.min(group, axis=0, keepdims=True)
        middle = 0.5 * (highest + lowest)
        spread = 0.5 * (highest - lowest) + EPSILON
        scale = 7.5 / spread
        size = spread * (1 / 7.5)
        codes = jnp.floor(jnp.clip(group * scale + (8.0 - middle * scale), 0.5, 15.5))
        restored = codes * size + (middle - 7.5 * size)
        results.append(restored.astype(jnp.bfloat16))
    return results


def quantize_kernel(weight, taken, synced, held, done):
    pairs, rows, block = held.shape
    width = min(PIECE, block)
    parity = lax.axis_index("tp") % 2
    copies = {}
    for pair in range(pairs):
        for start in range(0, block, width):
            at = pl.ds(pl.multiple_of((2 * pair + parity) * block + start, HD), width)
            copies[pair, start] = pltpu.make_async_copy(
                weight.at[:, at],
                held.at[pair, :, start : start + width],
                done.at[pair, start // width],
            )
            copies[pair, start].start()
    across = lax.broadcasted_iota(jnp.int32, (width, width), 0)
    along = lax.broadcasted_iota(jnp.int32, (width, width), 1)
    identity = jnp.where(across == along, 1.0, 0.0).astype(jnp.bfloat16)
    for own in (False, True):
        holder = parity if own else 1 - parity
        for pair in range(pairs):
            for start in range(0, block, width):
                if own:
                    copies[pair, start].wait()
                    entries = held[pair, :, start : start + width]
                else:
                    at = (2 * pair + parity) * block + start
                    entries = taken[:, pl.ds(pl.multiple_of(at, HD), width)]
                for index, result in enumerate(restore(entries, identity)):
                    at = pair * block + start + index * HD
                    synced[holder, at : at + HD] = result


def quantize(weight, taken, pairs):
    rows, width = weight.shape
    block = width // (2 * pairs)
    return pl.pallas_call(
        quantize_kernel,
        out_shape=jax.ShapeDtypeStruct((2, pairs * block, rows), jnp.bfloat16),
        in_specs=[pl.BlockSpec(memory_space=pltpu.HBM), in_vmem()],
        out_specs=in_vmem(),
        scratch_shapes=[
            pltpu.VMEM((pairs, rows, block), weight.dtype),
            pltpu.SemaphoreType.DMA((pairs, pl.cdiv(block, PIECE))),
        ],
        compiler_params=GRANT,
        name="quantize",
    )(in_hbm(weight), taken)


def project_kernel(order, distances, synced, *refs):
    replicas = len(order)
    states, outs = refs[:replicas], refs[replicas:]
    width = outs[0].shape[2]
    rows = synced.shape[2]
    pair = lax.axis_index("tp") // 2
    stacked = [as_rows(states[order.index(hop)][...]) for hop in range(replicas)]
    stacked = jnp.concatenate(stacked, axis=0)
    for distance, out in zip(distances, outs):
        at = pl.ds(pl.multiple_of((pair ^ distance) * width, width), width)
        part = sum(
            lax.dot_general(
                stacked[:, core * rows : (core + 1) * rows],
                synced[core, at, :],
                LANES_LAST,
                preferred_element_type=jnp.float32,
            )
            for core in range(2)
        )
        out[...] = part.astype(out.dtype).reshape(out.shape)


def project(synced, states, pairs, distances, dtype):
    order = visits(len(states), SENDING)
    tokens = states[0].shape[0] * states[0].shape[1]
    width = synced.shape[1] // pairs
    shape = jax.ShapeDtypeStruct((len(states), tokens, width), dtype)
    return pl.pallas_call(
        functools.partial(project_kernel, order, distances),
        out_shape=(shape,) * len(distances),
        in_specs=[in_vmem()] * (1 + len(states)),
        out_specs=(in_vmem(),) * len(distances),
        compiler_params=GRANT,
        name="project",
    )(synced, *[states[hop] for hop in order])


def weigh_kernel(table, lengths, query, keys, asked, weights, peaks, totals, wide):
    steps, rows, width = query.shape
    tokens = steps * rows
    heads = keys.shape[2] // HD
    group = width // (heads * HD)
    block = keys.shape[1]
    blocks = table.shape[1]
    factor = 1.0 / math.sqrt(HD)
    for member in range(heads * group):
        lanes = slice(member * HD, (member + 1) * HD)
        every = query[:, :, lanes].astype(jnp.float32).reshape(tokens, HD)
        wide[member * tokens : (member + 1) * tokens] = every
        asked[member * tokens : (member + 1) * tokens] = every.astype(jnp.bfloat16)
    for row in range(rows):
        length = lengths[row]
        for head in range(heads):
            lanes = slice(head * HD, (head + 1) * HD)
            at = pl.ds(head * group * tokens + row, group * steps, stride=rows)
            stacked = wide[at, :].astype(jnp.bfloat16)
            scores = []
            for part in range(blocks):
                score = lax.dot_general(
                    stacked,
                    keys[table[row, part], :, lanes],
                    LANES_LAST,
                    preferred_element_type=jnp.float32,
                )
                position = lax.broadcasted_iota(jnp.int32, (1, block), 1) + part * block
                scores.append(jnp.where(position < length, score * factor, -jnp.inf))
            peak = functools.reduce(
                jnp.maximum, [jnp.max(score, axis=1, keepdims=True) for score in scores]
            )
            total = jnp.zeros_like(peak)
            for part in range(blocks):
                weight = jnp.exp(scores[part] - peak)
                total = total + jnp.sum(weight, axis=1, keepdims=True)
                weights[row * heads + head, :, part * block : (part + 1) * block] = weight.astype(
                    jnp.bfloat16
                )
            peaks[at, :] = jnp.broadcast_to(peak, (group * steps, HD))
            totals[at, :] = jnp.broadcast_to(total, (group * steps, HD))


def weigh(table, lengths, query, keys):
    steps, rows, width = query.shape
    heads = keys.shape[2] // HD
    shape = (query.size // HD, HD)
    result = jax.ShapeDtypeStruct(shape, jnp.float32)
    span = table.shape[1] * keys.shape[1]
    weights = (rows * heads, steps * width // (heads * HD), span)
    return pl.pallas_call(
        weigh_kernel,
        out_shape=(
            jax.ShapeDtypeStruct(shape, jnp.bfloat16),
            jax.ShapeDtypeStruct(weights, jnp.bfloat16),
            result,
            result,
        ),
        in_specs=[in_smem()] * 2 + [in_vmem()] * 2,
        out_specs=(in_vmem(),) * 4,
        scratch_shapes=[pltpu.VMEM(shape, jnp.float32)],
        compiler_params=GRANT,
        name="weigh",
    )(table, lengths, query, keys)


def mix_kernel(table, weights, values, mixed):
    rows, blocks = table.shape
    block = values.shape[1]
    heads = values.shape[2] // HD
    asking = weights.shape[1]
    for row in range(rows):
        for head in range(heads):
            mix = jnp.zeros((asking, HD), jnp.float32)
            for part in range(blocks):
                mix = mix + jnp.dot(
                    weights[row * heads + head, :, part * block : (part + 1) * block],
                    values[table[row, part], :, head * HD : (head + 1) * HD],
                    preferred_element_type=jnp.float32,
                )
            mixed[pl.ds(head * asking * rows + row, asking, stride=rows), :] = mix


def mix(table, weights, values):
    shape = (weights.shape[0] * weights.shape[1], HD)
    return pl.pallas_call(
        mix_kernel,
        out_shape=jax.ShapeDtypeStruct(shape, jnp.float32),
        in_specs=[in_smem()] + [in_vmem()] * 2,
        out_specs=in_vmem(),
        compiler_params=GRANT,
        name="mix",
    )(table, weights, values)


def finish_kernel(kept, asked, mixed, peaks, totals, *refs):
    parts, (fresh, attended) = refs[:-2], refs[-2:]
    steps, rows, width = attended.shape
    tokens = steps * rows
    heads = fresh.shape[2] // (2 * HD)
    group = width // (heads * HD)
    factor = 1.0 / math.sqrt(HD)
    total = kept[...]
    for part in parts:
        total = total + part[...].astype(jnp.float32)
    entries = total.astype(jnp.bfloat16)
    fresh[...] = entries.astype(jnp.float32).reshape(fresh.shape).astype(jnp.bfloat16)
    shape = (group * tokens, tokens)
    asking = lax.broadcasted_iota(jnp.int32, shape, 0) % tokens
    told = lax.broadcasted_iota(jnp.int32, shape, 1)
    allowed = (asking % rows == told % rows) & (told <= asking)
    for head in range(heads):
        key = entries[:, 2 * head * HD : (2 * head + 1) * HD]
        value = entries[:, (2 * head + 1) * HD : (2 * head + 2) * HD]
        at = slice(head * group * tokens, (head + 1) * group * tokens)
        score = lax.dot_general(asked[at], key, LANES_LAST, preferred_element_type=jnp.float32)
        score = jnp.where(allowed, score * factor, -jnp.inf)
        before = peaks[at]
        peak = jnp.maximum(before, jnp.max(score, axis=1, keepdims=True))
        weight = jnp.exp(score - peak[:, :tokens])
        shrink = jnp.exp(before - peak)
        mix = mixed[at] * shrink + jnp.dot(
            weight.astype(jnp.bfloat16), value, preferred_element_type=jnp.float32
        )
        sums = totals[at] * shrink + jnp.sum(weight, axis=1, keepdims=True)
        result = mix / sums
        for member in range(group):
            lanes = slice((head * group + member) * HD, (head * group + member + 1) * HD)
            some = result[member * tokens : (member + 1) * tokens]
            attended[:, :, lanes] = some.reshape(steps, rows, HD).astype(jnp.bfloat16)


def finish(kept, parts, asked, mixed, peaks, totals, shape):
    return pl.pallas_call(
        finish_kernel,
        out_shape=(
            jax.ShapeDtypeStruct(shape[:2] + kept.shape[1:], jnp.bfloat16),
            jax.ShapeDtypeStruct(shape, jnp.bfloat16),
        ),
        in_specs=[in_vmem()] * (5 + len(parts)),
        out_specs=(in_vmem(), in_vmem()),
        compiler_params=GRANT,
        name="finish",
    )(kept, asked, mixed, peaks, totals, *parts)


def body(learner_weight, hidden_states, queries, cache_keys, cache_values, block_table, lengths):
    shard_rows = learner_weight.shape[0]
    replicas, across = lax.axis_size("fsdp"), lax.axis_size("tp")
    pairs = across // 2

    def swap(array, axis, distance):
        count = lax.axis_size(axis)
        return lax.ppermute(array, axis, [(i, i ^ distance) for i in range(count)])

    taken = swap(learner_weight, "tp", 1)
    states = list(collect(hidden_states, 2 * shard_rows, replicas))
    for hop in range(1, replicas):
        states[hop] = swap(states[hop], "fsdp", hop)
    synced = quantize(learner_weight, taken, pairs)
    half = pairs // 2
    given = project(synced, states, pairs, range(half, pairs), jnp.bfloat16)
    parts = list(project(synced, states, pairs, range(half), jnp.float32))
    parts += given
    asked, weights, peaks, totals = weigh(block_table, lengths, queries, cache_keys)
    while len(parts) > 1:
        half = len(parts) // 2
        moved = swap(jnp.stack(parts[half:]).astype(jnp.bfloat16), "tp", 2 * half)
        moved, block_table = lax.optimization_barrier((moved, block_table))
        parts = [
            part + moved[index].astype(jnp.float32) for index, part in enumerate(parts[:half])
        ]
    sums = parts[0]
    arrived = [
        swap(sums[hop].astype(jnp.bfloat16), "fsdp", hop)
        for hop in visits(replicas, RETURNING)
        if hop
    ]
    mixed = mix(block_table, weights, cache_values)
    return finish(sums[0], arrived, asked, mixed, peaks, totals, queries.shape)


def solution(mesh):
    return jax.shard_map(
        body,
        mesh=mesh,
        in_specs=(
            P(("groups", "fsdp", "tp"), None),
            P("groups", "fsdp", None),
            P("groups", "fsdp", "tp"),
            P(("groups", "fsdp"), None, "tp"),
            P(("groups", "fsdp"), None, "tp"),
            P(("groups", "fsdp"), None),
            P(("groups", "fsdp")),
        ),
        out_specs=(P("groups", "fsdp", "tp"), P("groups", "fsdp", "tp")),
        check_vma=False,
    )
```

```python
import functools
import math

import jax
import jax.numpy as jnp
from jax import lax
from jax.experimental import pallas as pl
from jax.experimental.pallas import tpu as pltpu
from jax.sharding import PartitionSpec as P

KVH = 8
HD = 128
EPSILON = 1e-06
PIECE = 256
SENDING = (2, 3, 1)
RETURNING = (3, 2, 1)
GRANT = pltpu.CompilerParams(vmem_limit_bytes=16 * 1024 * 1024)
LANES_LAST = (((1,), (1,)), ((), ()))


def in_vmem():
    return pl.BlockSpec(memory_space=pltpu.VMEM)


def in_smem():
    return pl.BlockSpec(memory_space=pltpu.SMEM)


def in_hbm(array):
    return pltpu.with_memory_space_constraint(array, pltpu.HBM)


def as_rows(block):
    return block.astype(jnp.float32).reshape(-1, block.shape[-1]).astype(block.dtype)


def visits(count, first):
    return [hop for hop in first if hop < count] + [hop for hop in range(count) if hop not in first]


def collect_kernel(states, *refs):
    blocks, done = refs[:-1], refs[-1]
    width = blocks[0].shape[2]
    replica, pair, pairs = lax.axis_index("fsdp"), lax.axis_index("tp") // 2, lax.axis_size("tp") // 2
    copies = []
    for hop, target in enumerate(blocks):
        start = pl.multiple_of(((replica ^ hop) * pairs + pair) * width, HD)
        source = states.at[:, :, pl.ds(start, width)]
        copies.append(pltpu.make_async_copy(source, target, done.at[hop]))
    for copy in copies[1:] + copies[:1]:
        copy.start()
    for copy in copies:
        copy.wait()


def collect(states, width, replicas):
    shape = states.shape[:2] + (width,)
    if width % HD:
        replica, pair, pairs = (
            lax.axis_index("fsdp"),
            lax.axis_index("tp") // 2,
            lax.axis_size("tp") // 2,
        )
        starts = [((replica ^ hop) * pairs + pair) * width for hop in range(replicas)]
        return [lax.dynamic_slice(states, (0, 0, start), shape) for start in starts]
    return pl.pallas_call(
        collect_kernel,
        out_shape=(jax.ShapeDtypeStruct(shape, states.dtype),) * replicas,
        in_specs=[pl.BlockSpec(memory_space=pltpu.HBM)],
        out_specs=(in_vmem(),) * replicas,
        scratch_shapes=[pltpu.SemaphoreType.DMA((replicas,))],
        compiler_params=GRANT,
        name="collect",
    )(in_hbm(states))


def restore(entries, identity):
    turned = lax.dot_general(identity, entries, LANES_LAST, preferred_element_type=jnp.float32)
    results = []
    for offset in range(0, turned.shape[0], HD):
        group = turned[offset : offset + HD]
        highest = jnp.max(group, axis=0, keepdims=True)
        lowest = jnp.min(group, axis=0, keepdims=True)
        middle = 0.5 * (highest + lowest)
        spread = 0.5 * (highest - lowest) + EPSILON
        scale = 7.5 / spread
        size = spread * (1 / 7.5)
        codes = jnp.floor(jnp.clip(group * scale + (8.0 - middle * scale), 0.5, 15.5))
        restored = codes * size + (middle - 7.5 * size)
        results.append(restored.astype(jnp.bfloat16))
    return results


def quantize_kernel(block, weight, taken, synced, held, done):
    rows, pairs = weight.shape[0], synced.shape[1] // block
    width = min(PIECE, block)
    depth = rows // done.shape[0]
    parity = lax.axis_index("tp") % 2
    copies = []
    for index in range(done.shape[0]):
        at = slice(index * depth, (index + 1) * depth)
        copies.append(pltpu.make_async_copy(weight.at[at], held.at[at], done.at[index]))
        copies[index].start()
    across = lax.broadcasted_iota(jnp.int32, (width, width), 0)
    along = lax.broadcasted_iota(jnp.int32, (width, width), 1)
    identity = jnp.where(across == along, 1.0, 0.0).astype(jnp.bfloat16)

    def fill(holder, source, some):
        for pair in range(pairs):
            for start in range(0, block, width):
                at = pl.multiple_of((2 * pair + parity) * block + start, HD)
                entries = source[some, pl.ds(at, width)]
                for index, result in enumerate(restore(entries, identity)):
                    at = pair * block + start + index * HD
                    synced[holder, at : at + HD, some] = result

    fill(1 - parity, taken, slice(0, rows))
    for index, copy in enumerate(copies):
        copy.wait()
        fill(parity, held, slice(index * depth, (index + 1) * depth))


def quantize(weight, taken, pairs):
    rows, width = weight.shape
    block = width // (2 * pairs)
    return pl.pallas_call(
        functools.partial(quantize_kernel, block),
        out_shape=jax.ShapeDtypeStruct((2, pairs * block, rows), jnp.bfloat16),
        in_specs=[pl.BlockSpec(memory_space=pltpu.HBM), in_vmem()],
        out_specs=in_vmem(),
        scratch_shapes=[
            pltpu.VMEM(weight.shape, weight.dtype),
            pltpu.SemaphoreType.DMA((pl.cdiv(rows, PIECE),)),
        ],
        compiler_params=GRANT,
        name="quantize",
    )(in_hbm(weight), taken)


def project_kernel(order, distances, synced, *refs):
    replicas = len(order)
    states, outs = refs[:replicas], refs[replicas:]
    width = outs[0].shape[2]
    rows = synced.shape[2]
    pair = lax.axis_index("tp") // 2
    stacked = [as_rows(states[order.index(hop)][...]) for hop in range(replicas)]
    stacked = jnp.concatenate(stacked, axis=0)
    for distance, out in zip(distances, outs):
        at = pl.ds(pl.multiple_of((pair ^ distance) * width, width), width)
        part = sum(
            lax.dot_general(
                stacked[:, core * rows : (core + 1) * rows],
                synced[core, at, :],
                LANES_LAST,
                preferred_element_type=jnp.float32,
            )
            for core in range(2)
        )
        out[...] = part.astype(out.dtype).reshape(out.shape)


def project(synced, states, pairs, distances, dtype):
    order = visits(len(states), SENDING)
    tokens = states[0].shape[0] * states[0].shape[1]
    width = synced.shape[1] // pairs
    shape = jax.ShapeDtypeStruct((len(states), tokens, width), dtype)
    return pl.pallas_call(
        functools.partial(project_kernel, order, distances),
        out_shape=(shape,) * len(distances),
        in_specs=[in_vmem()] * (1 + len(states)),
        out_specs=(in_vmem(),) * len(distances),
        compiler_params=GRANT,
        name="project",
    )(synced, *[states[hop] for hop in order])


def weigh_kernel(table, lengths, query, keys, asked, weights, peaks, totals, wide):
    steps, rows, width = query.shape
    tokens = steps * rows
    heads = keys.shape[2] // HD
    group = width // (heads * HD)
    block = keys.shape[1]
    blocks = table.shape[1]
    factor = 1.0 / math.sqrt(HD)
    for member in range(heads * group):
        lanes = slice(member * HD, (member + 1) * HD)
        every = query[:, :, lanes].astype(jnp.float32).reshape(tokens, HD)
        wide[member * tokens : (member + 1) * tokens] = every
        asked[member * tokens : (member + 1) * tokens] = every.astype(jnp.bfloat16)
    for row in range(rows):
        length = lengths[row]
        for head in range(heads):
            lanes = slice(head * HD, (head + 1) * HD)
            at = pl.ds(head * group * tokens + row, group * steps, stride=rows)
            stacked = wide[at, :].astype(jnp.bfloat16)
            scores = []
            for part in range(blocks):
                score = lax.dot_general(
                    stacked,
                    keys[table[row, part], :, lanes],
                    LANES_LAST,
                    preferred_element_type=jnp.float32,
                )
                position = lax.broadcasted_iota(jnp.int32, (1, block), 1) + part * block
                scores.append(jnp.where(position < length, score * factor, -jnp.inf))
            peak = functools.reduce(
                jnp.maximum, [jnp.max(score, axis=1, keepdims=True) for score in scores]
            )
            total = jnp.zeros_like(peak)
            for part in range(blocks):
                weight = jnp.exp(scores[part] - peak)
                total = total + jnp.sum(weight, axis=1, keepdims=True)
                weights[row * heads + head, :, part * block : (part + 1) * block] = weight.astype(
                    jnp.bfloat16
                )
            peaks[at, :] = jnp.broadcast_to(peak, (group * steps, HD))
            totals[at, :] = jnp.broadcast_to(total, (group * steps, HD))


def weigh(table, lengths, query, keys):
    steps, rows, width = query.shape
    heads = keys.shape[2] // HD
    shape = (query.size // HD, HD)
    result = jax.ShapeDtypeStruct(shape, jnp.float32)
    span = table.shape[1] * keys.shape[1]
    weights = (rows * heads, steps * width // (heads * HD), span)
    return pl.pallas_call(
        weigh_kernel,
        out_shape=(
            jax.ShapeDtypeStruct(shape, jnp.bfloat16),
            jax.ShapeDtypeStruct(weights, jnp.bfloat16),
            result,
            result,
        ),
        in_specs=[in_smem()] * 2 + [in_vmem()] * 2,
        out_specs=(in_vmem(),) * 4,
        scratch_shapes=[pltpu.VMEM(shape, jnp.float32)],
        compiler_params=GRANT,
        name="weigh",
    )(table, lengths, query, keys)


def mix_kernel(table, weights, values, mixed):
    rows, blocks = table.shape
    block = values.shape[1]
    heads = values.shape[2] // HD
    asking = weights.shape[1]
    for row in range(rows):
        for head in range(heads):
            mix = jnp.zeros((asking, HD), jnp.float32)
            for part in range(blocks):
                mix = mix + jnp.dot(
                    weights[row * heads + head, :, part * block : (part + 1) * block],
                    values[table[row, part], :, head * HD : (head + 1) * HD],
                    preferred_element_type=jnp.float32,
                )
            mixed[pl.ds(head * asking * rows + row, asking, stride=rows), :] = mix


def mix(table, weights, values):
    shape = (weights.shape[0] * weights.shape[1], HD)
    return pl.pallas_call(
        mix_kernel,
        out_shape=jax.ShapeDtypeStruct(shape, jnp.float32),
        in_specs=[in_smem()] + [in_vmem()] * 2,
        out_specs=in_vmem(),
        compiler_params=GRANT,
        name="mix",
    )(table, weights, values)


def finish_kernel(kept, asked, mixed, peaks, totals, *refs):
    parts, (fresh, attended) = refs[:-2], refs[-2:]
    steps, rows, width = attended.shape
    tokens = steps * rows
    heads = fresh.shape[2] // (2 * HD)
    group = width // (heads * HD)
    factor = 1.0 / math.sqrt(HD)
    total = kept[...]
    for part in parts:
        total = total + part[...].astype(jnp.float32)
    entries = total.astype(jnp.bfloat16)
    fresh[...] = entries.astype(jnp.float32).reshape(fresh.shape).astype(jnp.bfloat16)
    shape = (group * tokens, tokens)
    asking = lax.broadcasted_iota(jnp.int32, shape, 0) % tokens
    told = lax.broadcasted_iota(jnp.int32, shape, 1)
    allowed = (asking % rows == told % rows) & (told <= asking)
    for head in range(heads):
        key = entries[:, 2 * head * HD : (2 * head + 1) * HD]
        value = entries[:, (2 * head + 1) * HD : (2 * head + 2) * HD]
        at = slice(head * group * tokens, (head + 1) * group * tokens)
        score = lax.dot_general(asked[at], key, LANES_LAST, preferred_element_type=jnp.float32)
        score = jnp.where(allowed, score * factor, -jnp.inf)
        before = peaks[at]
        peak = jnp.maximum(before, jnp.max(score, axis=1, keepdims=True))
        weight = jnp.exp(score - peak[:, :tokens])
        shrink = jnp.exp(before - peak)
        mix = mixed[at] * shrink + jnp.dot(
            weight.astype(jnp.bfloat16), value, preferred_element_type=jnp.float32
        )
        sums = totals[at] * shrink + jnp.sum(weight, axis=1, keepdims=True)
        result = mix / sums
        for member in range(group):
            lanes = slice((head * group + member) * HD, (head * group + member + 1) * HD)
            some = result[member * tokens : (member + 1) * tokens]
            attended[:, :, lanes] = some.reshape(steps, rows, HD).astype(jnp.bfloat16)


def finish(kept, parts, asked, mixed, peaks, totals, shape):
    return pl.pallas_call(
        finish_kernel,
        out_shape=(
            jax.ShapeDtypeStruct(shape[:2] + kept.shape[1:], jnp.bfloat16),
            jax.ShapeDtypeStruct(shape, jnp.bfloat16),
        ),
        in_specs=[in_vmem()] * (5 + len(parts)),
        out_specs=(in_vmem(), in_vmem()),
        compiler_params=GRANT,
        name="finish",
    )(kept, asked, mixed, peaks, totals, *parts)


def body(learner_weight, hidden_states, queries, cache_keys, cache_values, block_table, lengths):
    shard_rows = learner_weight.shape[0]
    replicas, across = lax.axis_size("fsdp"), lax.axis_size("tp")
    pairs = across // 2

    def swap(array, axis, distance):
        count = lax.axis_size(axis)
        return lax.ppermute(array, axis, [(i, i ^ distance) for i in range(count)])

    taken = swap(learner_weight, "tp", 1)
    states = list(collect(hidden_states, 2 * shard_rows, replicas))
    for hop in range(1, replicas):
        states[hop] = swap(states[hop], "fsdp", hop)
    synced = quantize(learner_weight, taken, pairs)
    half = pairs // 2
    given = project(synced, states, pairs, range(half, pairs), jnp.bfloat16)
    parts = list(project(synced, states, pairs, range(half), jnp.float32))
    parts, lengths = lax.optimization_barrier((parts, lengths))
    parts += given
    asked, weights, peaks, totals = weigh(block_table, lengths, queries, cache_keys)
    while len(parts) > 1:
        half = len(parts) // 2
        moved = swap(jnp.stack(parts[half:]).astype(jnp.bfloat16), "tp", 2 * half)
        moved, block_table = lax.optimization_barrier((moved, block_table))
        parts = [
            part + moved[index].astype(jnp.float32) for index, part in enumerate(parts[:half])
        ]
    sums = parts[0]
    arrived = [
        swap(sums[hop].astype(jnp.bfloat16), "fsdp", hop)
        for hop in visits(replicas, RETURNING)
        if hop
    ]
    mixed = mix(block_table, weights, cache_values)
    return finish(sums[0], arrived, asked, mixed, peaks, totals, queries.shape)


def solution(mesh):
    return jax.shard_map(
        body,
        mesh=mesh,
        in_specs=(
            P(("groups", "fsdp", "tp"), None),
            P("groups", "fsdp", None),
            P("groups", "fsdp", "tp"),
            P(("groups", "fsdp"), None, "tp"),
            P(("groups", "fsdp"), None, "tp"),
            P(("groups", "fsdp"), None),
            P(("groups", "fsdp")),
        ),
        out_specs=(P("groups", "fsdp", "tp"), P("groups", "fsdp", "tp")),
        check_vma=False,
    )
```

```python
import functools
import math

import jax
import jax.numpy as jnp
from jax import lax
from jax.experimental import pallas as pl
from jax.experimental.pallas import tpu as pltpu
from jax.sharding import PartitionSpec as P

KVH = 8
HD = 128
EPSILON = 1e-06
PIECE = 256
SENDING = (2, 3, 1)
RETURNING = (3, 2, 1)
GRANT = pltpu.CompilerParams(vmem_limit_bytes=16 * 1024 * 1024)
LANES_LAST = (((1,), (1,)), ((), ()))


def in_vmem():
    return pl.BlockSpec(memory_space=pltpu.VMEM)


def in_smem():
    return pl.BlockSpec(memory_space=pltpu.SMEM)


def in_hbm(array):
    return pltpu.with_memory_space_constraint(array, pltpu.HBM)


def as_rows(block):
    return block.astype(jnp.float32).reshape(-1, block.shape[-1]).astype(block.dtype)


def visits(count, first):
    return [hop for hop in first if hop < count] + [hop for hop in range(count) if hop not in first]


def collect_kernel(states, *refs):
    blocks, done = refs[:-1], refs[-1]
    width = blocks[0].shape[2]
    replica, pair, pairs = lax.axis_index("fsdp"), lax.axis_index("tp") // 2, lax.axis_size("tp") // 2
    copies = []
    for hop, target in enumerate(blocks):
        start = pl.multiple_of(((replica ^ hop) * pairs + pair) * width, HD)
        source = states.at[:, :, pl.ds(start, width)]
        copies.append(pltpu.make_async_copy(source, target, done.at[hop]))
    for copy in copies[1:] + copies[:1]:
        copy.start()
    for copy in copies:
        copy.wait()


def collect(states, width, replicas):
    shape = states.shape[:2] + (width,)
    if width % HD:
        replica, pair, pairs = (
            lax.axis_index("fsdp"),
            lax.axis_index("tp") // 2,
            lax.axis_size("tp") // 2,
        )
        starts = [((replica ^ hop) * pairs + pair) * width for hop in range(replicas)]
        return [lax.dynamic_slice(states, (0, 0, start), shape) for start in starts]
    return pl.pallas_call(
        collect_kernel,
        out_shape=(jax.ShapeDtypeStruct(shape, states.dtype),) * replicas,
        in_specs=[pl.BlockSpec(memory_space=pltpu.HBM)],
        out_specs=(in_vmem(),) * replicas,
        scratch_shapes=[pltpu.SemaphoreType.DMA((replicas,))],
        compiler_params=GRANT,
        name="collect",
    )(in_hbm(states))


def restore(entries, identity):
    turned = lax.dot_general(identity, entries, LANES_LAST, preferred_element_type=jnp.float32)
    results = []
    for offset in range(0, turned.shape[0], HD):
        group = turned[offset : offset + HD]
        highest = jnp.max(group, axis=0, keepdims=True)
        lowest = jnp.min(group, axis=0, keepdims=True)
        middle = 0.5 * (highest + lowest)
        spread = 0.5 * (highest - lowest) + EPSILON
        scale = 7.5 / spread
        size = spread * (1 / 7.5)
        codes = jnp.floor(jnp.clip(group * scale + (8.0 - middle * scale), 0.5, 15.5))
        restored = codes * size + (middle - 7.5 * size)
        results.append(restored.astype(jnp.bfloat16))
    return results


def quantize_kernel(block, weight, taken, synced, held, done):
    rows, pairs = weight.shape[0], synced.shape[1] // block
    width = min(PIECE, block)
    depth = rows // done.shape[0]
    parity = lax.axis_index("tp") % 2
    copies = []
    for index in range(done.shape[0]):
        at = slice(index * depth, (index + 1) * depth)
        copies.append(pltpu.make_async_copy(weight.at[at], held.at[at], done.at[index]))
        copies[index].start()
    across = lax.broadcasted_iota(jnp.int32, (width, width), 0)
    along = lax.broadcasted_iota(jnp.int32, (width, width), 1)
    identity = jnp.where(across == along, 1.0, 0.0).astype(jnp.bfloat16)

    def fill(holder, source, some):
        for pair in range(pairs):
            for start in range(0, block, width):
                at = pl.multiple_of((2 * pair + parity) * block + start, HD)
                entries = source[some, pl.ds(at, width)]
                for index, result in enumerate(restore(entries, identity)):
                    at = pair * block + start + index * HD
                    synced[holder, at : at + HD, some] = result

    fill(1 - parity, taken, slice(0, rows))
    for index, copy in enumerate(copies):
        copy.wait()
        fill(parity, held, slice(index * depth, (index + 1) * depth))


def quantize(weight, taken, pairs):
    rows, width = weight.shape
    block = width // (2 * pairs)
    return pl.pallas_call(
        functools.partial(quantize_kernel, block),
        out_shape=jax.ShapeDtypeStruct((2, pairs * block, rows), jnp.bfloat16),
        in_specs=[pl.BlockSpec(memory_space=pltpu.HBM), in_vmem()],
        out_specs=in_vmem(),
        scratch_shapes=[
            pltpu.VMEM(weight.shape, weight.dtype),
            pltpu.SemaphoreType.DMA((pl.cdiv(rows, PIECE),)),
        ],
        compiler_params=GRANT,
        name="quantize",
    )(in_hbm(weight), taken)


def project_kernel(order, distances, synced, *refs):
    replicas = len(order)
    states, outs = refs[:replicas], refs[replicas:]
    width = outs[0].shape[2]
    rows = synced.shape[2]
    pair = lax.axis_index("tp") // 2
    stacked = [as_rows(states[order.index(hop)][...]) for hop in range(replicas)]
    stacked = jnp.concatenate(stacked, axis=0)
    for distance, out in zip(distances, outs):
        at = pl.ds(pl.multiple_of((pair ^ distance) * width, width), width)
        part = sum(
            lax.dot_general(
                stacked[:, core * rows : (core + 1) * rows],
                synced[core, at, :],
                LANES_LAST,
                preferred_element_type=jnp.float32,
            )
            for core in range(2)
        )
        out[...] = part.astype(out.dtype).reshape(out.shape)


def project(synced, states, pairs, distances, dtype):
    order = visits(len(states), SENDING)
    tokens = states[0].shape[0] * states[0].shape[1]
    width = synced.shape[1] // pairs
    shape = jax.ShapeDtypeStruct((len(states), tokens, width), dtype)
    return pl.pallas_call(
        functools.partial(project_kernel, order, distances),
        out_shape=(shape,) * len(distances),
        in_specs=[in_vmem()] * (1 + len(states)),
        out_specs=(in_vmem(),) * len(distances),
        compiler_params=GRANT,
        name="project",
    )(synced, *[states[hop] for hop in order])


def weigh_kernel(table, lengths, query, keys, asked, weights, peaks, totals, wide):
    steps, rows, width = query.shape
    tokens = steps * rows
    heads = keys.shape[2] // HD
    group = width // (heads * HD)
    block = keys.shape[1]
    blocks = table.shape[1]
    factor = 1.0 / math.sqrt(HD)
    for member in range(heads * group):
        lanes = slice(member * HD, (member + 1) * HD)
        every = query[:, :, lanes].astype(jnp.float32).reshape(tokens, HD)
        wide[member * tokens : (member + 1) * tokens] = every
        asked[member * tokens : (member + 1) * tokens] = every.astype(jnp.bfloat16)
    for row in range(rows):
        length = lengths[row]
        for head in range(heads):
            lanes = slice(head * HD, (head + 1) * HD)
            at = pl.ds(head * group * tokens + row, group * steps, stride=rows)
            stacked = wide[at, :].astype(jnp.bfloat16)
            scores = []
            for part in range(blocks):
                score = lax.dot_general(
                    stacked,
                    keys[table[row, part], :, lanes],
                    LANES_LAST,
                    preferred_element_type=jnp.float32,
                )
                position = lax.broadcasted_iota(jnp.int32, (1, block), 1) + part * block
                scores.append(jnp.where(position < length, score * factor, -jnp.inf))
            peak = functools.reduce(
                jnp.maximum, [jnp.max(score, axis=1, keepdims=True) for score in scores]
            )
            total = jnp.zeros_like(peak)
            for part in range(blocks):
                weight = jnp.exp(scores[part] - peak)
                total = total + jnp.sum(weight, axis=1, keepdims=True)
                weights[row * heads + head, :, part * block : (part + 1) * block] = weight.astype(
                    jnp.bfloat16
                )
            peaks[at, :] = jnp.broadcast_to(peak, (group * steps, HD))
            totals[at, :] = jnp.broadcast_to(total, (group * steps, HD))


def weigh(table, lengths, query, keys):
    steps, rows, width = query.shape
    heads = keys.shape[2] // HD
    shape = (query.size // HD, HD)
    result = jax.ShapeDtypeStruct(shape, jnp.float32)
    span = table.shape[1] * keys.shape[1]
    weights = (rows * heads, steps * width // (heads * HD), span)
    return pl.pallas_call(
        weigh_kernel,
        out_shape=(
            jax.ShapeDtypeStruct(shape, jnp.bfloat16),
            jax.ShapeDtypeStruct(weights, jnp.bfloat16),
            result,
            result,
        ),
        in_specs=[in_smem()] * 2 + [in_vmem()] * 2,
        out_specs=(in_vmem(),) * 4,
        scratch_shapes=[pltpu.VMEM(shape, jnp.float32)],
        compiler_params=GRANT,
        name="weigh",
    )(table, lengths, query, keys)


def mix_kernel(table, weights, values, mixed):
    rows, blocks = table.shape
    block = values.shape[1]
    heads = values.shape[2] // HD
    asking = weights.shape[1]
    for row in range(rows):
        for head in range(heads):
            mix = jnp.zeros((asking, HD), jnp.float32)
            for part in range(blocks):
                mix = mix + jnp.dot(
                    weights[row * heads + head, :, part * block : (part + 1) * block],
                    values[table[row, part], :, head * HD : (head + 1) * HD],
                    preferred_element_type=jnp.float32,
                )
            mixed[pl.ds(head * asking * rows + row, asking, stride=rows), :] = mix


def mix(table, weights, values):
    shape = (weights.shape[0] * weights.shape[1], HD)
    return pl.pallas_call(
        mix_kernel,
        out_shape=jax.ShapeDtypeStruct(shape, jnp.float32),
        in_specs=[in_smem()] + [in_vmem()] * 2,
        out_specs=in_vmem(),
        compiler_params=GRANT,
        name="mix",
    )(table, weights, values)


def finish_kernel(kept, asked, mixed, peaks, totals, *refs):
    parts, (fresh_out, attended_out, fresh, attended, done) = refs[:-5], refs[-5:]
    steps, rows, width = attended.shape
    tokens = steps * rows
    heads = fresh.shape[2] // (2 * HD)
    group = width // (heads * HD)
    factor = 1.0 / math.sqrt(HD)
    total = kept[...]
    for part in parts:
        total = total + part[...].astype(jnp.float32)
    entries = total.astype(jnp.bfloat16)
    fresh[...] = entries.astype(jnp.float32).reshape(fresh.shape).astype(jnp.bfloat16)
    copies = [pltpu.make_async_copy(fresh, fresh_out, done.at[heads])]
    copies[0].start()
    shape = (group * tokens, tokens)
    asking = lax.broadcasted_iota(jnp.int32, shape, 0) % tokens
    told = lax.broadcasted_iota(jnp.int32, shape, 1)
    allowed = (asking % rows == told % rows) & (told <= asking)
    for head in range(heads):
        key = entries[:, 2 * head * HD : (2 * head + 1) * HD]
        value = entries[:, (2 * head + 1) * HD : (2 * head + 2) * HD]
        at = slice(head * group * tokens, (head + 1) * group * tokens)
        score = lax.dot_general(asked[at], key, LANES_LAST, preferred_element_type=jnp.float32)
        score = jnp.where(allowed, score * factor, -jnp.inf)
        before = peaks[at]
        peak = jnp.maximum(before, jnp.max(score, axis=1, keepdims=True))
        weight = jnp.exp(score - peak[:, :tokens])
        shrink = jnp.exp(before - peak)
        mix = mixed[at] * shrink + jnp.dot(
            weight.astype(jnp.bfloat16), value, preferred_element_type=jnp.float32
        )
        sums = totals[at] * shrink + jnp.sum(weight, axis=1, keepdims=True)
        result = mix / sums
        for member in range(group):
            lanes = slice((head * group + member) * HD, (head * group + member + 1) * HD)
            some = result[member * tokens : (member + 1) * tokens]
            attended[:, :, lanes] = some.reshape(steps, rows, HD).astype(jnp.bfloat16)
        lanes = slice(head * group * HD, (head + 1) * group * HD)
        copies.append(
            pltpu.make_async_copy(
                attended.at[:, :, lanes], attended_out.at[:, :, lanes], done.at[head]
            )
        )
        copies[-1].start()
    for copy in copies:
        copy.wait()


def finish(kept, parts, asked, mixed, peaks, totals, shape):
    return pl.pallas_call(
        finish_kernel,
        out_shape=(
            jax.ShapeDtypeStruct(shape[:2] + kept.shape[1:], jnp.bfloat16),
            jax.ShapeDtypeStruct(shape, jnp.bfloat16),
        ),
        in_specs=[in_vmem()] * (5 + len(parts)),
        out_specs=(pl.BlockSpec(memory_space=pltpu.HBM),) * 2,
        scratch_shapes=[
            pltpu.VMEM(shape[:2] + kept.shape[1:], jnp.bfloat16),
            pltpu.VMEM(shape, jnp.bfloat16),
            pltpu.SemaphoreType.DMA((kept.shape[1] // (2 * HD) + 1,)),
        ],
        compiler_params=GRANT,
        name="finish",
    )(kept, asked, mixed, peaks, totals, *parts)


def body(learner_weight, hidden_states, queries, cache_keys, cache_values, block_table, lengths):
    shard_rows = learner_weight.shape[0]
    replicas, across = lax.axis_size("fsdp"), lax.axis_size("tp")
    pairs = across // 2

    def swap(array, axis, distance):
        count = lax.axis_size(axis)
        return lax.ppermute(array, axis, [(i, i ^ distance) for i in range(count)])

    taken = swap(learner_weight, "tp", 1)
    states = list(collect(hidden_states, 2 * shard_rows, replicas))
    for hop in range(1, replicas):
        states[hop] = swap(states[hop], "fsdp", hop)
    synced = quantize(learner_weight, taken, pairs)
    half = pairs // 2
    given = project(synced, states, pairs, range(half, pairs), jnp.bfloat16)
    parts = list(project(synced, states, pairs, range(half), jnp.float32))
    parts, lengths = lax.optimization_barrier((parts, lengths))
    parts += given
    asked, weights, peaks, totals = weigh(block_table, lengths, queries, cache_keys)
    while len(parts) > 1:
        half = len(parts) // 2
        moved = swap(jnp.stack(parts[half:]).astype(jnp.bfloat16), "tp", 2 * half)
        moved, block_table = lax.optimization_barrier((moved, block_table))
        parts = [
            part + moved[index].astype(jnp.float32) for index, part in enumerate(parts[:half])
        ]
    sums = parts[0]
    arrived = [
        swap(sums[hop].astype(jnp.bfloat16), "fsdp", hop)
        for hop in visits(replicas, RETURNING)
        if hop
    ]
    mixed = mix(block_table, weights, cache_values)
    return finish(sums[0], arrived, asked, mixed, peaks, totals, queries.shape)


def solution(mesh):
    return jax.shard_map(
        body,
        mesh=mesh,
        in_specs=(
            P(("groups", "fsdp", "tp"), None),
            P("groups", "fsdp", None),
            P("groups", "fsdp", "tp"),
            P(("groups", "fsdp"), None, "tp"),
            P(("groups", "fsdp"), None, "tp"),
            P(("groups", "fsdp"), None),
            P(("groups", "fsdp")),
        ),
        out_specs=(P("groups", "fsdp", "tp"), P("groups", "fsdp", "tp")),
        check_vma=False,
    )
```

```python
import functools
import math

import jax
import jax.numpy as jnp
from jax import lax
from jax.experimental import pallas as pl
from jax.experimental.pallas import tpu as pltpu
from jax.sharding import PartitionSpec as P

KVH = 8
HD = 128
EPSILON = 1e-06
PIECE = 256
SENDING = (2, 3, 1)
RETURNING = (3, 2, 1)
GRANT = pltpu.CompilerParams(vmem_limit_bytes=16 * 1024 * 1024)
LANES_LAST = (((1,), (1,)), ((), ()))


def in_vmem():
    return pl.BlockSpec(memory_space=pltpu.VMEM)


def in_smem():
    return pl.BlockSpec(memory_space=pltpu.SMEM)


def in_hbm(array):
    return pltpu.with_memory_space_constraint(array, pltpu.HBM)


def as_rows(block):
    return jnp.concatenate([block[step] for step in range(block.shape[0])], axis=0)


def visits(count, first):
    return [hop for hop in first if hop < count] + [hop for hop in range(count) if hop not in first]


def collect_kernel(states, *refs):
    blocks, done = refs[:-1], refs[-1]
    width = blocks[0].shape[2]
    replica, pair, pairs = lax.axis_index("fsdp"), lax.axis_index("tp") // 2, lax.axis_size("tp") // 2
    copies = []
    for hop, target in enumerate(blocks):
        start = pl.multiple_of(((replica ^ hop) * pairs + pair) * width, HD)
        source = states.at[:, :, pl.ds(start, width)]
        copies.append(pltpu.make_async_copy(source, target, done.at[hop]))
    for copy in copies[1:] + copies[:1]:
        copy.start()
    for copy in copies:
        copy.wait()


def collect(states, width, replicas):
    shape = states.shape[:2] + (width,)
    if width % HD:
        replica, pair, pairs = (
            lax.axis_index("fsdp"),
            lax.axis_index("tp") // 2,
            lax.axis_size("tp") // 2,
        )
        starts = [((replica ^ hop) * pairs + pair) * width for hop in range(replicas)]
        return [lax.dynamic_slice(states, (0, 0, start), shape) for start in starts]
    return pl.pallas_call(
        collect_kernel,
        out_shape=(jax.ShapeDtypeStruct(shape, states.dtype),) * replicas,
        in_specs=[pl.BlockSpec(memory_space=pltpu.HBM)],
        out_specs=(in_vmem(),) * replicas,
        scratch_shapes=[pltpu.SemaphoreType.DMA((replicas,))],
        compiler_params=GRANT,
        name="collect",
    )(in_hbm(states))


def restore(entries, identity):
    turned = lax.dot_general(identity, entries, LANES_LAST, preferred_element_type=jnp.float32)
    results = []
    for offset in range(0, turned.shape[0], HD):
        group = turned[offset : offset + HD]
        highest = jnp.max(group, axis=0, keepdims=True)
        lowest = jnp.min(group, axis=0, keepdims=True)
        middle = 0.5 * (highest + lowest)
        spread = 0.5 * (highest - lowest) + EPSILON
        scale = 7.5 / spread
        size = spread * (1 / 7.5)
        codes = jnp.floor(jnp.clip(group * scale + (8.0 - middle * scale), 0.5, 15.5))
        restored = codes * size + (middle - 7.5 * size)
        results.append(restored.astype(jnp.bfloat16))
    return results


def quantize_kernel(block, weight, taken, synced, held, done):
    rows, pairs = weight.shape[0], synced.shape[1] // block
    width = min(PIECE, block)
    depth = rows // done.shape[0]
    parity = lax.axis_index("tp") % 2
    copies = []
    for index in range(done.shape[0]):
        at = slice(index * depth, (index + 1) * depth)
        copies.append(pltpu.make_async_copy(weight.at[at], held.at[at], done.at[index]))
        copies[index].start()
    across = lax.broadcasted_iota(jnp.int32, (width, width), 0)
    along = lax.broadcasted_iota(jnp.int32, (width, width), 1)
    identity = jnp.where(across == along, 1.0, 0.0).astype(jnp.bfloat16)

    def fill(holder, source, some):
        for pair in range(pairs):
            for start in range(0, block, width):
                at = pl.multiple_of((2 * pair + parity) * block + start, HD)
                entries = source[some, pl.ds(at, width)]
                for index, result in enumerate(restore(entries, identity)):
                    at = pair * block + start + index * HD
                    synced[holder, at : at + HD, some] = result

    fill(1 - parity, taken, slice(0, rows))
    for index, copy in enumerate(copies):
        copy.wait()
        fill(parity, held, slice(index * depth, (index + 1) * depth))


def quantize(weight, taken, pairs):
    rows, width = weight.shape
    block = width // (2 * pairs)
    return pl.pallas_call(
        functools.partial(quantize_kernel, block),
        out_shape=jax.ShapeDtypeStruct((2, pairs * block, rows), jnp.bfloat16),
        in_specs=[pl.BlockSpec(memory_space=pltpu.HBM), in_vmem()],
        out_specs=in_vmem(),
        scratch_shapes=[
            pltpu.VMEM(weight.shape, weight.dtype),
            pltpu.SemaphoreType.DMA((pl.cdiv(rows, PIECE),)),
        ],
        compiler_params=GRANT,
        name="quantize",
    )(in_hbm(weight), taken)


def project_kernel(order, distances, synced, *refs):
    replicas = len(order)
    states, outs = refs[:replicas], refs[replicas:]
    width = outs[0].shape[2]
    rows = synced.shape[2]
    pair = lax.axis_index("tp") // 2
    stacked = [as_rows(states[order.index(hop)][...]) for hop in range(replicas)]
    stacked = jnp.concatenate(stacked, axis=0)
    for distance, out in zip(distances, outs):
        at = pl.ds(pl.multiple_of((pair ^ distance) * width, width), width)
        part = sum(
            lax.dot_general(
                stacked[:, core * rows : (core + 1) * rows],
                synced[core, at, :],
                LANES_LAST,
                preferred_element_type=jnp.float32,
            )
            for core in range(2)
        )
        out[...] = part.astype(out.dtype).reshape(out.shape)


def project(synced, states, pairs, distances, dtype):
    order = visits(len(states), SENDING)
    tokens = states[0].shape[0] * states[0].shape[1]
    width = synced.shape[1] // pairs
    shape = jax.ShapeDtypeStruct((len(states), tokens, width), dtype)
    return pl.pallas_call(
        functools.partial(project_kernel, order, distances),
        out_shape=(shape,) * len(distances),
        in_specs=[in_vmem()] * (1 + len(states)),
        out_specs=(in_vmem(),) * len(distances),
        compiler_params=GRANT,
        name="project",
    )(synced, *[states[hop] for hop in order])


def weigh_kernel(table, lengths, query, keys, asked, weights, peaks, totals, wide):
    steps, rows, width = query.shape
    tokens = steps * rows
    heads = keys.shape[2] // HD
    group = width // (heads * HD)
    block = keys.shape[1]
    blocks = table.shape[1]
    factor = 1.0 / math.sqrt(HD)
    for member in range(heads * group):
        lanes = slice(member * HD, (member + 1) * HD)
        every = query[:, :, lanes].astype(jnp.float32).reshape(tokens, HD)
        wide[member * tokens : (member + 1) * tokens] = every
        asked[member * tokens : (member + 1) * tokens] = every.astype(jnp.bfloat16)
    for row in range(rows):
        length = lengths[row]
        for head in range(heads):
            lanes = slice(head * HD, (head + 1) * HD)
            at = pl.ds(head * group * tokens + row, group * steps, stride=rows)
            stacked = wide[at, :].astype(jnp.bfloat16)
            scores = []
            for part in range(blocks):
                score = lax.dot_general(
                    stacked,
                    keys[table[row, part], :, lanes],
                    LANES_LAST,
                    preferred_element_type=jnp.float32,
                )
                position = lax.broadcasted_iota(jnp.int32, (1, block), 1) + part * block
                scores.append(jnp.where(position < length, score * factor, -jnp.inf))
            peak = functools.reduce(
                jnp.maximum, [jnp.max(score, axis=1, keepdims=True) for score in scores]
            )
            total = jnp.zeros_like(peak)
            for part in range(blocks):
                weight = jnp.exp(scores[part] - peak)
                total = total + jnp.sum(weight, axis=1, keepdims=True)
                weights[row * heads + head, :, part * block : (part + 1) * block] = weight.astype(
                    jnp.bfloat16
                )
            peaks[at, :] = jnp.broadcast_to(peak, (group * steps, HD))
            totals[at, :] = jnp.broadcast_to(total, (group * steps, HD))


def weigh(table, lengths, query, keys):
    steps, rows, width = query.shape
    heads = keys.shape[2] // HD
    shape = (query.size // HD, HD)
    result = jax.ShapeDtypeStruct(shape, jnp.float32)
    span = table.shape[1] * keys.shape[1]
    weights = (rows * heads, steps * width // (heads * HD), span)
    return pl.pallas_call(
        weigh_kernel,
        out_shape=(
            jax.ShapeDtypeStruct(shape, jnp.bfloat16),
            jax.ShapeDtypeStruct(weights, jnp.bfloat16),
            result,
            result,
        ),
        in_specs=[in_smem()] * 2 + [in_vmem()] * 2,
        out_specs=(in_vmem(),) * 4,
        scratch_shapes=[pltpu.VMEM(shape, jnp.float32)],
        compiler_params=GRANT,
        name="weigh",
    )(table, lengths, query, keys)


def mix_kernel(table, weights, values, mixed):
    rows, blocks = table.shape
    block = values.shape[1]
    heads = values.shape[2] // HD
    asking = weights.shape[1]
    for row in range(rows):
        for head in range(heads):
            mix = jnp.zeros((asking, HD), jnp.float32)
            for part in range(blocks):
                mix = mix + jnp.dot(
                    weights[row * heads + head, :, part * block : (part + 1) * block],
                    values[table[row, part], :, head * HD : (head + 1) * HD],
                    preferred_element_type=jnp.float32,
                )
            mixed[pl.ds(head * asking * rows + row, asking, stride=rows), :] = mix


def mix(table, weights, values):
    shape = (weights.shape[0] * weights.shape[1], HD)
    return pl.pallas_call(
        mix_kernel,
        out_shape=jax.ShapeDtypeStruct(shape, jnp.float32),
        in_specs=[in_smem()] + [in_vmem()] * 2,
        out_specs=in_vmem(),
        compiler_params=GRANT,
        name="mix",
    )(table, weights, values)


def finish_kernel(kept, asked, mixed, peaks, totals, *refs):
    parts, (fresh, attended) = refs[:-2], refs[-2:]
    steps, rows, width = attended.shape
    tokens = steps * rows
    heads = fresh.shape[2] // (2 * HD)
    group = width // (heads * HD)
    factor = 1.0 / math.sqrt(HD)
    total = kept[...]
    for part in parts:
        total = total + part[...].astype(jnp.float32)
    entries = total.astype(jnp.bfloat16)
    fresh[...] = entries.astype(jnp.float32).reshape(fresh.shape).astype(jnp.bfloat16)
    shape = (group * tokens, tokens)
    asking = lax.broadcasted_iota(jnp.int32, shape, 0) % tokens
    told = lax.broadcasted_iota(jnp.int32, shape, 1)
    allowed = (asking % rows == told % rows) & (told <= asking)
    for head in range(heads):
        key = entries[:, 2 * head * HD : (2 * head + 1) * HD]
        value = entries[:, (2 * head + 1) * HD : (2 * head + 2) * HD]
        at = slice(head * group * tokens, (head + 1) * group * tokens)
        score = lax.dot_general(asked[at], key, LANES_LAST, preferred_element_type=jnp.float32)
        score = jnp.where(allowed, score * factor, -jnp.inf)
        before = peaks[at]
        peak = jnp.maximum(before, jnp.max(score, axis=1, keepdims=True))
        weight = jnp.exp(score - peak[:, :tokens])
        shrink = jnp.exp(before - peak)
        mix = mixed[at] * shrink + jnp.dot(
            weight.astype(jnp.bfloat16), value, preferred_element_type=jnp.float32
        )
        sums = totals[at] * shrink + jnp.sum(weight, axis=1, keepdims=True)
        result = mix / sums
        for member in range(group):
            lanes = slice((head * group + member) * HD, (head * group + member + 1) * HD)
            some = result[member * tokens : (member + 1) * tokens]
            attended[:, :, lanes] = some.reshape(steps, rows, HD).astype(jnp.bfloat16)


def finish(kept, parts, asked, mixed, peaks, totals, shape):
    return pl.pallas_call(
        finish_kernel,
        out_shape=(
            jax.ShapeDtypeStruct(shape[:2] + kept.shape[1:], jnp.bfloat16),
            jax.ShapeDtypeStruct(shape, jnp.bfloat16),
        ),
        in_specs=[in_vmem()] * (5 + len(parts)),
        out_specs=(in_vmem(), in_vmem()),
        compiler_params=GRANT,
        name="finish",
    )(kept, asked, mixed, peaks, totals, *parts)


def body(learner_weight, hidden_states, queries, cache_keys, cache_values, block_table, lengths):
    shard_rows = learner_weight.shape[0]
    replicas, across = lax.axis_size("fsdp"), lax.axis_size("tp")
    pairs = across // 2

    def swap(array, axis, distance):
        count = lax.axis_size(axis)
        return lax.ppermute(array, axis, [(i, i ^ distance) for i in range(count)])

    taken = swap(learner_weight, "tp", 1)
    states = list(collect(hidden_states, 2 * shard_rows, replicas))
    for hop in range(1, replicas):
        states[hop] = swap(states[hop], "fsdp", hop)
    synced = quantize(learner_weight, taken, pairs)
    half = pairs // 2
    given = project(synced, states, pairs, range(half, pairs), jnp.bfloat16)
    parts = list(project(synced, states, pairs, range(half), jnp.float32))
    parts, lengths = lax.optimization_barrier((parts, lengths))
    parts += given
    asked, weights, peaks, totals = weigh(block_table, lengths, queries, cache_keys)
    while len(parts) > 1:
        half = len(parts) // 2
        moved = swap(jnp.stack(parts[half:]).astype(jnp.bfloat16), "tp", 2 * half)
        moved, block_table = lax.optimization_barrier((moved, block_table))
        parts = [
            part + moved[index].astype(jnp.float32) for index, part in enumerate(parts[:half])
        ]
    sums = parts[0]
    arrived = [
        swap(sums[hop].astype(jnp.bfloat16), "fsdp", hop)
        for hop in visits(replicas, RETURNING)
        if hop
    ]
    mixed = mix(block_table, weights, cache_values)
    return finish(sums[0], arrived, asked, mixed, peaks, totals, queries.shape)


def solution(mesh):
    return jax.shard_map(
        body,
        mesh=mesh,
        in_specs=(
            P(("groups", "fsdp", "tp"), None),
            P("groups", "fsdp", None),
            P("groups", "fsdp", "tp"),
            P(("groups", "fsdp"), None, "tp"),
            P(("groups", "fsdp"), None, "tp"),
            P(("groups", "fsdp"), None),
            P(("groups", "fsdp")),
        ),
        out_specs=(P("groups", "fsdp", "tp"), P("groups", "fsdp", "tp")),
        check_vma=False,
    )
```
